512 devices in a mesh: tile: 64 (over x, z), grp: 8 (over y, core).
Axes of the slice: x: 4, y: 4, z: 16, core: 2. Of those that a mesh axis runs over, the one named last changes fastest.
Arguments:
- visibilities: bfloat16 [64, 8, 64, 32, 512], P('tile', 'grp'), may hold values from -6 to 6
- channel_taps: bfloat16 [64, 8, 64, 8, 256], P('tile', 'grp'), may hold values from 0.099609375 to 1
- time_taps: bfloat16 [64, 8, 64, 8, 32], P('tile', 'grp'), may hold values from 0.099609375 to 1
- channel_shift: int32 [64, 8, 64, 256], P('tile', 'grp'), may hold values from 0 to 56
- time_shift: int32 [64, 8, 64, 32], P('tile', 'grp'), may hold values from 0 to 56
- corner: int32 [64, 8, 64, 2], P('tile', 'grp'), may hold values from 0 to 127
- plane_index: int32 [64, 8, 64], P('tile', 'grp'), may hold values from 0 to 7
- owner_tile: int32 [64, 8, 64], P('tile', 'grp'), may hold values from 0 to 63, as said below
Outputs:
- grid: float32 [8, 2, 8192, 1024], P(None, None, 'tile', 'grp')
The draws below stay inside these ranges and needn't reach their ends.
Inputs may be any that keep to these rules, and one draw needn't show every extreme that they name: Among the 64 entries of owner_tile[i, h] no tile appears more than 2 times; for each h one tile appears exactly 2 times in owner_tile[i, h] for every i.
All inputs are finite; a program needn't handle non-finite values.
Results may differ from the reference program's by a relative error of at most 0.0029.
Values may be sent and summed in bfloat16 or wider, within the bound.
A program may use at most 64 MiB of HBM per device.

```python
import jax
import jax.numpy as jnp
from jax import lax

CH = 256
TM = 32
TAPS = 8
PATCH = 64
TILE = 128
PLANES = 8
PER = 8
CT = 2
BLK_DEV = 64
NR = 8192
NC = 1024
N_TILE = 64
N_GRP = 8


def draw_owner_tile(key, part):
    key = jax.random.fold_in(key, 7)
    rows = N_GRP * PER
    hot_key, rest = jax.random.split(key)
    hot = jax.random.randint(hot_key, (N_GRP,), 0, N_TILE)
    hots = jnp.tile(hot, N_TILE)

    def one_group(group_key, hot_tile):
        first, second = jax.random.split(group_key)
        scores = jax.random.permutation(first, N_TILE).astype(jnp.int32)
        scores = jnp.where(jnp.arange(N_TILE) == hot_tile, -1, scores)
        order = jnp.argsort(scores, stable=True).astype(jnp.int32)
        chosen = order[jnp.arange(rows) // CT]
        return jax.random.permutation(second, chosen)
    keys = jax.random.split(rest, N_TILE * N_GRP)
    drawn = jax.vmap(one_group)(keys, hots)
    return drawn.reshape(N_TILE, N_GRP, rows).astype(jnp.int32)


def with_ends(values, stream_key, low, largest):
    index_at = [jax.random.randint(jax.random.fold_in(stream_key, axis), (), 0, length) for axis, length in enumerate(values.shape)]
    longest = values.shape.index(max(values.shape))
    next_to = index_at[:longest] + [(index_at[longest] + 1) % values.shape[longest]] + index_at[longest + 1:]
    return values.at[tuple(index_at)].set(low).at[tuple(next_to)].set(largest)


def block_levels(stream_key, shape, cuts, least, largest):
    level = 1.0
    for position, parts in cuts:
        steps = jax.random.uniform(jax.random.fold_in(jax.random.fold_in(stream_key, 6), position), (parts,), jnp.float32, least / len(cuts), largest / len(cuts))
        level = level * jnp.repeat(jnp.exp(steps), shape[position] // parts).reshape((-1,) + (1,) * (len(shape) - 1 - position))
    return level


def bell_draw(key, shape, scale, bound, cuts=(), kind=jnp.bfloat16):
    values = scale * jax.random.normal(key, shape, jnp.float32)
    if cuts:
        values = values * block_levels(key, shape, cuts, -0.22, 0.18)
    return jnp.clip(values, -bound, bound).astype(kind)


def setup_inputs(seed: int = 0) -> dict:
    splits = jax.random.split(jax.random.key(seed), 9)
    return {
        "visibilities": bell_draw(splits[0], (N_TILE, N_GRP, BLK_DEV, TM, 2 * CH), 1.0, 6.0, ((0, 64), (1, 8))),
        "channel_taps": jnp.clip(0.099609375 + 0.9003906 * jax.random.uniform(splits[1], (N_TILE, N_GRP, BLK_DEV, TAPS, CH), jnp.float32) ** block_levels(splits[1], (N_TILE, N_GRP, BLK_DEV, TAPS, CH), ((0, 64), (1, 8)), -0.2, 0.2), 0.099609375, 1.0).astype(jnp.bfloat16),
        "time_taps": jnp.clip(0.099609375 + 0.9003906 * jax.random.uniform(splits[2], (N_TILE, N_GRP, BLK_DEV, TAPS, TM), jnp.float32) ** block_levels(splits[2], (N_TILE, N_GRP, BLK_DEV, TAPS, TM), ((0, 64), (1, 8)), -0.2, 0.2), 0.099609375, 1.0).astype(jnp.bfloat16),
        "channel_shift": with_ends(jax.random.randint(splits[3], (N_TILE, N_GRP, BLK_DEV, CH), 0, PATCH - TAPS + 1), jax.random.fold_in(splits[3], 1), 0, PATCH - TAPS).astype(jnp.int32),
        "time_shift": with_ends(jax.random.randint(splits[4], (N_TILE, N_GRP, BLK_DEV, TM), 0, PATCH - TAPS + 1), jax.random.fold_in(splits[4], 1), 0, PATCH - TAPS).astype(jnp.int32),
        "corner": with_ends(jax.random.randint(splits[5], (N_TILE, N_GRP, BLK_DEV, 2), 0, TILE), jax.random.fold_in(splits[5], 1), 0, TILE - 1).astype(jnp.int32),
        "plane_index": with_ends(jax.random.randint(splits[6], (N_TILE, N_GRP, BLK_DEV), 0, PLANES), jax.random.fold_in(splits[6], 1), 0, PLANES - 1).astype(jnp.int32),
        "owner_tile": draw_owner_tile(jax.random.fold_in(splits[8], 71), 0),
    }


def kernel_matrix(taps, shift, extent):
    cells = jnp.arange(extent, dtype=jnp.int32)
    total = jnp.zeros(shift.shape + (extent,), jnp.float32)
    for index in range(taps.shape[1]):
        hit = cells[None, None, :] == (shift + index)[:, :, None]
        total = total + jnp.where(hit, taps[:, index, :, None].astype(jnp.float32), jnp.float32(0.0))
    return total.astype(jnp.bfloat16)


def block_patches(samples, row_taps, col_taps, placing):
    width = row_taps.shape[-1]
    span = col_taps.shape[-1]
    row_kernel = kernel_matrix(row_taps, placing[:, :width], PATCH)
    col_kernel = kernel_matrix(col_taps, placing[:, width:width + span], PATCH)
    folded = jnp.einsum("stc,stq->sqc", samples.astype(jnp.float32), col_kernel.astype(jnp.float32)).astype(jnp.bfloat16)
    folded = folded.reshape(folded.shape[0], PATCH, 2, width)
    return jnp.einsum("scp,sqxc->sxpq", row_kernel.astype(jnp.float32), folded.astype(jnp.float32))


def reference(visibilities, channel_taps, time_taps, channel_shift, time_shift, corner, plane_index, owner_tile):
    sources = N_TILE * N_GRP
    rows = BLK_DEV
    base = CH + TM
    placing = jnp.concatenate([channel_shift, time_shift, corner, plane_index[..., None]], axis=-1)
    placing = placing.reshape(sources, rows, base + 3)
    samples = visibilities.reshape(sources, rows, TM, 2 * CH)
    row_taps = channel_taps.reshape(sources, rows, TAPS, CH)
    col_taps = time_taps.reshape(sources, rows, TAPS, TM)
    tiles = owner_tile.reshape(N_TILE, N_GRP, N_GRP, PER).transpose(0, 2, 1, 3).reshape(sources, rows)
    band = (jnp.arange(rows, dtype=jnp.int32) // PER).astype(jnp.int32)
    padded = jnp.zeros((PLANES, 2, NR + PATCH, NC + PATCH), jnp.float32)

    def one_source(current, pieces):
        block_samples, block_rows, block_cols, place, owner = pieces
        made = block_patches(block_samples, block_rows, block_cols, place)
        row_start = (owner * TILE + place[:, base]).astype(jnp.int32)
        col_start = (band * TILE + place[:, base + 1]).astype(jnp.int32)

        def add_one(index, grid_now):
            start = (place[index, base + 2], jnp.int32(0), row_start[index], col_start[index])
            old = lax.dynamic_slice(grid_now, start, (1, 2, PATCH, PATCH))
            return lax.dynamic_update_slice(grid_now, old + made[index][None], start)

        return lax.fori_loop(0, rows, add_one, current), None

    padded, _ = lax.scan(one_source, padded, (samples, row_taps, col_taps, placing, tiles))
    result = padded[:, :, :NR, :NC]
    result = result.at[:, :, :PATCH, :].add(padded[:, :, NR:, :NC])
    result = result.at[:, :, :, :PATCH].add(padded[:, :, :NR, NC:])
    result = result.at[:, :, :PATCH, :PATCH].add(padded[:, :, NR:, NC:])
    return result
```

```python
import functools

import jax
import jax.numpy as jnp
from jax import lax
from jax.experimental import pallas as pl
from jax.experimental.pallas import tpu as pltpu
from jax.sharding import PartitionSpec as P

PATCH = 64
TILE = 128
PLANES = 8
CT = 2
TM = 32
CH = 256
GROWS = 32
MROWS = 16
BROWS = GROWS + MROWS
PROWS = 2 * GROWS + MROWS
MAIN = PLANES * TILE
SIDE = PLANES * PATCH
f32 = jnp.float32
bf16 = jnp.bfloat16
VMEM = pltpu.VMEM
SMEM = pltpu.SMEM


def params(**kw):
    return pltpu.CompilerParams(vmem_limit_bytes=40 * 1024 * 1024, **kw)


def rotated(taps, low):
    for bit in (1, 2, 4):
        taps = jnp.where((low & bit) != 0, pltpu.roll(taps, bit, 0), taps)
    return taps


def fold_kernel(steps, corner, plane, vis, ctaps, ttaps, cshift, tshift, out):
    base = pl.program_id(0) * steps
    sub = lax.broadcasted_iota(jnp.int32, (8, CH), 0)
    sub1 = lax.broadcasted_iota(jnp.int32, (8, 128), 0)
    for b in range(steps):
        c0 = corner[base + b, 0]
        c1 = corner[base + b, 1]
        at = jnp.broadcast_to((cshift[b : b + 1, :] + c0) & (PATCH - 1), (8, CH))
        low = at & 7
        turned = rotated(ctaps[b].astype(f32), low)
        group = ((at >> 3) + jnp.where(sub < low, 1, 0)) & 7
        rows = jnp.concatenate(
            [jnp.where(group == r, turned, 0.0) for r in range(PATCH // 8)], axis=0
        ).astype(bf16)
        both = jnp.concatenate([vis[b, :, :CH], vis[b, :, CH:]], axis=0)
        made = lax.dot_general(both, rows, (((1,), (1,)), ((), ())), preferred_element_type=f32)
        out[b, :GROWS, :] = jnp.concatenate([made[:TM], made[TM:]], axis=1).astype(bf16)
        wide = jnp.concatenate([ttaps[b].astype(f32)] * 4, axis=1)
        shift = jnp.concatenate([tshift[b : b + 1, :] + c1] * 4, axis=1)
        shift = jnp.broadcast_to(shift, (8, 128))
        rest = jnp.where(
            sub1 == 0, shift, jnp.where(sub1 == 1, plane[base + b], jnp.where(sub1 == 2, c0, 0))
        )
        out[b, GROWS:, :] = jnp.concatenate([wide, rest.astype(f32)], axis=0).astype(bf16)


def fold(vis, ctaps, ttaps, cshift, tshift, corner, plane):
    blocks, steps = vis.shape[0], 8

    def spec(a):
        rest = a.shape[1:]
        return pl.BlockSpec((steps,) + rest, lambda i: (i,) + (0,) * len(rest))

    smem = pl.BlockSpec(memory_space=SMEM)
    return pl.pallas_call(
        functools.partial(fold_kernel, steps),
        grid=(blocks // steps,),
        out_shape=jax.ShapeDtypeStruct((blocks, BROWS, 128), bf16),
        in_specs=[smem, smem] + [spec(a) for a in (vis, ctaps, ttaps, cshift, tshift)],
        out_specs=pl.BlockSpec((steps, BROWS, 128), lambda i: (i, 0, 0)),
        compiler_params=params(),
    )(corner, plane, vis, ctaps, ttaps, cshift, tshift)


def pack_kernel(blocks, source, held, out):
    lane = lax.broadcasted_iota(jnp.int32, (MROWS, 128), 1)
    first = (lane & 63) < 32

    def one(j, _):
        a, b = source[2 * j], source[2 * j + 1]
        ia, ib = jnp.minimum(a, blocks - 1), jnp.minimum(b, blocks - 1)
        out[j, :GROWS, :] = held[ia, :GROWS, :]
        out[j, GROWS : 2 * GROWS, :] = held[ib, :GROWS, :]
        ma = jnp.where(a < blocks, held[ia, GROWS:, :].astype(f32), 0.0)
        mb = jnp.where(b < blocks, held[ib, GROWS:, :].astype(f32), 0.0)
        out[j, 2 * GROWS :, :] = jnp.where(first, ma, mb).astype(bf16)
        return 0

    lax.fori_loop(0, out.shape[0], one, 0, unroll=4)


def pack(source, held, tiles):
    return pl.pallas_call(
        functools.partial(pack_kernel, held.shape[0]),
        out_shape=jax.ShapeDtypeStruct((tiles, PROWS, 128), bf16),
        in_specs=[pl.BlockSpec(memory_space=SMEM), pl.BlockSpec(memory_space=VMEM)],
        out_specs=pl.BlockSpec(memory_space=VMEM),
        compiler_params=params(),
    )(source, held)


def place_batch(msgs, first):
    lane = lax.broadcasted_iota(jnp.int32, (MROWS, 128), 1)
    sub = lax.broadcasted_iota(jnp.int32, (8, 128), 0)
    prow = lax.broadcasted_iota(jnp.int32, (128, 128), 0) & (PATCH - 1)
    lhs, rhs = [], []
    for q in range(2):
        a, b = first + 2 * q, first + 2 * q + 1
        meta = jnp.where(
            lane < 64,
            msgs[a, 2 * GROWS :, :].astype(f32),
            msgs[b, 2 * GROWS :, :].astype(f32),
        )
        taps = meta[:8]
        ints = meta[8:].astype(jnp.int32)
        at = jnp.broadcast_to(ints[0:1], (8, 128))
        level = jnp.broadcast_to(ints[1:2], (8, 128))
        low = at & 7
        turned = rotated(taps, low)
        group = (at >> 3) + jnp.where(sub < low, 1, 0)
        group = jnp.where(group < 16, level * 16 + group, 112 + level * 8 + group)
        rhs.append(
            jnp.concatenate(
                [jnp.where(group == r, turned, 0.0).astype(bf16) for r in range(192)], axis=0
            )
        )
        g = jnp.concatenate([msgs[a, : 2 * GROWS, :], msgs[b, : 2 * GROWS, :]], axis=0)
        g = jnp.transpose(g.astype(f32))
        off = prow - ints[2:3]
        lhs.append(
            jnp.concatenate(
                [
                    jnp.where((off >= -64 * k) & (off < 64 - 64 * k), g, 0.0).astype(bf16)
                    for k in range(3)
                ],
                axis=0,
            )
        )
    return jnp.concatenate(lhs, axis=1), jnp.concatenate(rhs, axis=1)


def place_kernel(msgs, inner, lower, right, corner):
    for ref in (inner, lower, right, corner):
        ref[...] = jnp.zeros_like(ref)

    def one(step, _):
        lhs, rhs = place_batch(msgs, step * 4)
        for n in range(0, MAIN + SIDE, 256):
            part = lax.dot_general(
                lhs, rhs[n : n + 256], (((1,), (1,)), ((), ())), preferred_element_type=f32
            )
            if n < MAIN:
                inner[:, n : n + 256] += part[:256]
                lower[:, n : n + 256] += part[256:]
            else:
                m = n - MAIN
                right[:, m : m + 256] += part[:256]
                corner[:, m : m + 256] += part[256:]
        return 0

    lax.fori_loop(0, msgs.shape[0] // 4, one, 0)


def place(msgs):
    vm = pl.BlockSpec(memory_space=VMEM)
    return pl.pallas_call(
        place_kernel,
        out_shape=[
            jax.ShapeDtypeStruct((256, MAIN), f32),
            jax.ShapeDtypeStruct((128, MAIN), f32),
            jax.ShapeDtypeStruct((256, SIDE), f32),
            jax.ShapeDtypeStruct((128, SIDE), f32),
        ],
        in_specs=[vm],
        out_specs=[vm] * 4,
        compiler_params=params(),
    )(msgs)


def join_kernel(inner, lower, right, corner, out):
    for n in range(PLANES):
        cols = slice(n * TILE, (n + 1) * TILE)
        side = slice(n * PATCH, (n + 1) * PATCH)
        for k in range(2):
            rows = slice(128 * k, 128 * (k + 1))
            main = inner[rows, cols]
            edge = right[rows, side]
            if k == 0:
                main = main + lower[:, cols]
                edge = edge + corner[:, side]
            main = main + jnp.concatenate([edge, jnp.zeros_like(edge)], axis=1)
            for x in range(2):
                out[n, x, 64 * k : 64 * (k + 1), :] = main[64 * x : 64 * (x + 1)]


def join(inner, lower, right, corner):
    vm = pl.BlockSpec(memory_space=VMEM)
    return pl.pallas_call(
        join_kernel,
        out_shape=jax.ShapeDtypeStruct((PLANES, 2, TILE, TILE), f32),
        in_specs=[vm] * 4,
        out_specs=vm,
        compiler_params=params(),
    )(inner, lower, right, corner)


def slot_sources(tiles, n_tile):
    rows = tiles.shape[0]
    order = jnp.arange(rows, dtype=jnp.int32)
    same = tiles[:, None] == tiles[None, :]
    rank = jnp.sum(jnp.where(same & (order[None, :] < order[:, None]), 1, 0), axis=1)
    slot_of = tiles * CT + rank.astype(jnp.int32)
    match = jnp.arange(n_tile * CT, dtype=jnp.int32)[:, None] == slot_of[None, :]
    return rows - jnp.sum(jnp.where(match, rows - order[None, :], 0), axis=1)


def shards(
    visibilities,
    channel_taps,
    time_taps,
    channel_shift,
    time_shift,
    corner,
    plane_index,
    owner_tile,
):
    n_grp = lax.axis_size("grp")
    n_tile = lax.axis_size("tile")
    rows = visibilities.shape[2]
    per = rows // n_grp
    source = slot_sources(owner_tile[0, 0], n_tile)
    folded = fold(
        visibilities[0, 0],
        channel_taps[0, 0],
        time_taps[0, 0],
        channel_shift[0, 0],
        time_shift[0, 0],
        corner[0, 0],
        plane_index[0, 0],
    )
    held = lax.all_to_all(
        folded.reshape(n_grp, per, BROWS, 128), "grp", split_axis=0, concat_axis=0, tiled=True
    ).reshape(rows, BROWS, 128)
    msgs = lax.all_to_all(
        pack(source, held, n_tile), "tile", split_axis=0, concat_axis=0, tiled=True
    )
    inner, lower, right, edge = place(msgs)
    down = [(i, (i + 1) % n_tile) for i in range(n_tile)]
    side = [(i, (i + 1) % n_grp) for i in range(n_grp)]
    both = [
        (i * n_grp + g, ((i + 1) % n_tile) * n_grp + (g + 1) % n_grp)
        for i in range(n_tile)
        for g in range(n_grp)
    ]
    lower = lax.ppermute(lower, "tile", down)
    right = lax.ppermute(right, "grp", side)
    edge = lax.ppermute(edge, ("tile", "grp"), both)
    return join(inner, lower, right, edge)


def solution(mesh):
    in_specs = (
        P("tile", "grp", None, None, None),
        P("tile", "grp", None, None, None),
        P("tile", "grp", None, None, None),
        P("tile", "grp", None, None),
        P("tile", "grp", None, None),
        P("tile", "grp", None, None),
        P("tile", "grp", None),
        P("tile", "grp", None),
    )
    out_specs = P(None, None, "tile", "grp")
    return jax.shard_map(shards, mesh=mesh, in_specs=in_specs, out_specs=out_specs, check_vma=False)
```

```python
import jax
import jax.numpy as jnp
from jax import lax
from jax.experimental import pallas as pl
from jax.experimental.pallas import tpu as pltpu
from jax.sharding import PartitionSpec as P

PATCH = 64
TILE = 128
PLANES = 8
CT = 2
TM = 32
CH = 256
N_X = 4
N_Z = 16
N_Y = 4
N_TILE = N_X * N_Z
N_GRP = 2 * N_Y
PER = 8
UNITS = PER + 1
MROWS = 16
PROWS = 2 * TM + MROWS
SELF_G = N_GRP - 1
SELF_T = N_TILE - N_X
MESH = pl.DeviceIdType.MESH
f32 = jnp.float32
bf16 = jnp.bfloat16


def rotated(taps, low):
    for bit in (1, 2, 4):
        taps = jnp.where((low & bit) != 0, pltpu.roll(taps, bit, 0), taps)
    return taps


def grp_at(grp, e, way):
    dy = lax.rem(lax.div(e, 2) + 1, N_Y)
    dc = 1 - lax.rem(e, 2)
    y = lax.rem(lax.div(grp, 2) + way * dy + N_Y, N_Y)
    return y * 2 + lax.rem(lax.rem(grp, 2) + dc, 2)


def tile_at(tile, k, way):
    dx = lax.rem(k, N_X)
    zi = lax.div(k, N_X)
    half = lax.div(zi + 1, 2)
    dz = N_Z // 2 + half * (1 - 2 * lax.rem(zi, 2))
    x = lax.rem(lax.div(tile, N_Z) + way * dx + N_X, N_X)
    return x * N_Z + lax.rem(lax.rem(tile, N_Z) + way * dz + N_Z, N_Z)


def place_batch(msgs, first):
    lane = lax.broadcasted_iota(jnp.int32, (MROWS, 128), 1)
    sub = lax.broadcasted_iota(jnp.int32, (8, 128), 0)
    prow = lax.broadcasted_iota(jnp.int32, (128, 128), 0) & (PATCH - 1)
    lhs, rhs = [], []
    for q in range(2):
        a, b = first + 2 * q, first + 2 * q + 1
        meta = jnp.where(
            lane < 64, msgs[a, 2 * TM :, :].astype(f32), msgs[b, 2 * TM :, :].astype(f32)
        )
        ints = meta[8:].astype(jnp.int32)
        at = jnp.broadcast_to(ints[0:1], (8, 128))
        level = jnp.broadcast_to(ints[1:2], (8, 128))
        low = at & 7
        turned = rotated(meta[:8], low)
        group = (at >> 3) + jnp.where(sub < low, 1, 0)
        group = (group >> 3) * 64 + level * 8 + (group & 7)
        rhs.append(
            jnp.concatenate(
                [jnp.where(group == r, turned, 0.0).astype(bf16) for r in range(192)], axis=0
            )
        )
        g = jnp.concatenate([msgs[a, : 2 * TM, :], msgs[b, : 2 * TM, :]], axis=0)
        g = jnp.transpose(g.astype(f32))
        off = prow - ints[2:3]
        lhs.append(
            jnp.concatenate(
                [
                    jnp.where((off >= -64 * k) & (off < 64 - 64 * k), g, 0.0).astype(bf16)
                    for k in range(3)
                ],
                axis=0,
            )
        )
    return jnp.concatenate(lhs, axis=1), jnp.concatenate(rhs, axis=1)


def grid_kernel(
    corner,
    plane,
    source,
    vis,
    ctaps,
    cshift,
    ttaps,
    tshift,
    out,
    vis_buf,
    ct_buf,
    cs_buf,
    gout,
    gin,
    meta_buf,
    tout,
    tin,
    acc,
    side_in,
    low0_in,
    low1_in,
    vis_sem,
    small_sem,
    gsend,
    grecv,
    tsend,
    trecv,
    side_sem,
    low0_sem,
    low1_sem,
):
    tile = lax.axis_index("tile")
    grp = lax.axis_index("grp")

    barrier = pltpu.get_barrier_semaphore()

    def greet_tile(k, _):
        @pl.when(k != SELF_T)
        def _():
            pl.semaphore_signal(
                barrier, inc=1, device_id=(tile_at(tile, k, 1), grp), device_id_type=MESH
            )

        return 0

    def greet_grp(e, _):
        pl.semaphore_signal(
            barrier, inc=1, device_id=(tile, grp_at(grp, e, 1)), device_id_type=MESH
        )
        return 0

    def vis_copy(e):
        base = pl.multiple_of(grp_at(grp, e, 1) * PER, PER)
        return pltpu.make_async_copy(
            vis.at[pl.ds(base, PER)], vis_buf.at[pl.ds(e * PER, PER)], vis_sem.at[e]
        )

    small = [
        pltpu.make_async_copy(ctaps, ct_buf, small_sem.at[0]),
        pltpu.make_async_copy(cshift, cs_buf, small_sem.at[1]),
    ]
    for copy in small:
        copy.start()

    def start_vis(e, _):
        vis_copy(e).start()
        return 0

    lax.fori_loop(0, N_GRP, start_vis, 0)
    lax.fori_loop(0, N_GRP - 1, greet_grp, 0)
    lax.fori_loop(0, N_TILE, greet_tile, 0)

    acc[...] = jnp.zeros_like(acc)
    meta_buf[PER] = jnp.zeros((MROWS, 128), f32)
    for copy in small:
        copy.wait()
    pl.semaphore_wait(barrier, N_TILE - 1 + N_GRP - 1)

    sub = lax.broadcasted_iota(jnp.int32, (8, CH), 0)
    sub1 = lax.broadcasted_iota(jnp.int32, (8, 128), 0)
    lane = lax.broadcasted_iota(jnp.int32, (MROWS, 128), 1)

    def grp_copy(e):
        units = pl.ds(e * UNITS, UNITS)
        return pltpu.make_async_remote_copy(
            src_ref=gout.at[units],
            dst_ref=gin.at[units],
            send_sem=gsend.at[e],
            recv_sem=grecv.at[e],
            device_id=(tile, grp_at(grp, e, 1)),
            device_id_type=MESH,
        )

    def fold(e, _):
        base = pl.multiple_of(grp_at(grp, e, 1) * PER, PER)
        vis_copy(e).wait()
        shifts = cs_buf[pl.ds(base, PER), :]
        tshifts = tshift[pl.ds(base, PER), :]
        metas = []
        for b in range(PER):
            c0 = corner[base + b, 0]
            c1 = corner[base + b, 1]
            at = jnp.broadcast_to((shifts[b : b + 1, :] + c0) & (PATCH - 1), (8, CH))
            low = at & 7
            if b % 2 == 0:
                two = ct_buf[pl.ds(pl.multiple_of(base * 8, 16) + b * 8, 16), :].astype(f32)
            turned = rotated(two[(b % 2) * 8 : (b % 2) * 8 + 8], low)
            group = ((at >> 3) + jnp.where(sub < low, 1, 0)) & 7
            rows = jnp.concatenate(
                [jnp.where(group == r, turned, 0.0) for r in range(PATCH // 8)], axis=0
            ).astype(bf16)
            samples = vis_buf[e * PER + b]
            both = jnp.concatenate([samples[:, :CH], samples[:, CH:]], axis=0)
            made = lax.dot_general(
                both, rows, (((1,), (1,)), ((), ())), preferred_element_type=f32
            )
            gout[e * UNITS + b] = jnp.concatenate([made[:TM], made[TM:]], axis=1).astype(bf16)
            wide = jnp.concatenate([ttaps[base + b].astype(f32)] * 4, axis=1)
            shift = jnp.concatenate([tshifts[b : b + 1, :] + c1] * 4, axis=1)
            rest = jnp.where(
                sub1 == 0,
                jnp.broadcast_to(shift, (8, 128)),
                jnp.where(sub1 == 1, plane[base + b], jnp.where(sub1 == 2, c0, 0)),
            )
            metas.append(jnp.concatenate([wide, rest.astype(f32)], axis=0))
        halves = []
        for half in range(2):
            four = metas[4 * half]
            for b in range(1, 4):
                four = jnp.where(lane < 32 * b, four, metas[4 * half + b])
            halves.append(four)
        gout[e * UNITS + PER] = jnp.concatenate(halves, axis=0).astype(bf16)

        @pl.when(e != SELF_G)
        def _():
            grp_copy(e).start()

        return 0

    lax.fori_loop(0, N_GRP, fold, 0)
    gin[SELF_G * UNITS :] = gout[SELF_G * UNITS :]

    def spread(e, _):
        @pl.when(e != SELF_G)
        def _():
            grp_copy(e).wait_recv()

        eight = gin[e * UNITS + PER].astype(f32)
        for b in range(PER):
            at = (b // 4) * MROWS
            own = (lane >= 32 * (b % 4)) & (lane < 32 * (b % 4) + 32)
            only = jnp.where(own, eight[at : at + MROWS], 0.0)
            only = only + pltpu.roll(only, 64, 1)
            meta_buf[e * UNITS + b] = only + pltpu.roll(only, 32, 1)
        return 0

    lax.fori_loop(0, N_GRP, spread, 0)

    def tile_copy(k):
        return pltpu.make_async_remote_copy(
            src_ref=tout.at[k],
            dst_ref=tin.at[k],
            send_sem=tsend.at[k],
            recv_sem=trecv.at[k],
            device_id=(tile_at(tile, k, 1), grp),
            device_id_type=MESH,
        )

    def pack(k, _):
        to = tile_at(tile, k, 1)
        a, b = source[2 * to], source[2 * to + 1]
        tout[k, :TM, :] = gin[a]
        tout[k, TM : 2 * TM, :] = gin[b]
        tout[k, 2 * TM :, :] = jnp.where((lane & 63) < 32, meta_buf[a], meta_buf[b]).astype(bf16)

        @pl.when(k != SELF_T)
        def _():
            tile_copy(k).start()

        return 0

    lax.fori_loop(0, N_TILE, pack, 0)
    tin[SELF_T] = tout[SELF_T]

    def place(step, _):
        for i in range(4):

            @pl.when(step * 4 + i != SELF_T)
            def _():
                tile_copy(step * 4 + i).wait_recv()

        lhs, rhs = place_batch(tin, step * 4)
        for n in range(6):
            part = lax.dot_general(
                lhs,
                rhs[256 * n : 256 * (n + 1)],
                (((1,), (1,)), ((), ())),
                preferred_element_type=f32,
            )
            acc[2 * n] += part[:, :128]
            acc[2 * n + 1] += part[:, 128:]
        return 0

    lax.fori_loop(0, N_TILE // 4, place, 0)

    down = lax.rem(tile + 1, N_TILE)
    right = lax.rem(grp + 1, N_GRP)
    side_copies = [
        pltpu.make_async_remote_copy(
            src_ref=acc.at[8 + c],
            dst_ref=side_in.at[c],
            send_sem=side_sem.at[0, c],
            recv_sem=side_sem.at[1, c],
            device_id=(tile, right),
            device_id_type=MESH,
        )
        for c in range(4)
    ]
    low1_copy = pltpu.make_async_remote_copy(
        src_ref=acc.at[pl.ds(4, 4), pl.ds(256, 128)],
        dst_ref=low1_in,
        send_sem=low1_sem.at[0],
        recv_sem=low1_sem.at[1],
        device_id=(down, grp),
        device_id_type=MESH,
    )
    low0_copies = [
        pltpu.make_async_remote_copy(
            src_ref=acc.at[c, pl.ds(256, 128)],
            dst_ref=low0_in.at[c],
            send_sem=low0_sem.at[0, c],
            recv_sem=low0_sem.at[1, c],
            device_id=(down, grp),
            device_id_type=MESH,
        )
        for c in range(4)
    ]
    for copy in side_copies:
        copy.start()
    low1_copy.start()
    for c in range(4):
        side_copies[c].wait_recv()
        acc[c] += side_in[c]
        low0_copies[c].start()

    def write(c, k, left, rest):
        for n in range(2):
            cols = slice(64 * n, 64 * (n + 1))
            both = jnp.concatenate([left[:, cols], rest[:, cols]], axis=1)
            for x in range(2):
                out[2 * c + n, x, 64 * k : 64 * (k + 1), :] = both[64 * x : 64 * (x + 1)]

    for c in range(4):
        write(c, 1, acc[c, 128:256], acc[4 + c, 128:256])
    low1_copy.wait_recv()
    for c in range(4):
        low0_copies[c].wait_recv()
        write(c, 0, acc[c, :128] + low0_in[c], acc[4 + c, :128] + low1_in[c])

    def sent_grp(e, _):
        grp_copy(e).wait_send()
        return 0

    def sent_tile(k, _):
        @pl.when(k != SELF_T)
        def _():
            tile_copy(k).wait_send()

        return 0

    lax.fori_loop(0, N_GRP - 1, sent_grp, 0)
    lax.fori_loop(0, N_TILE, sent_tile, 0)
    low1_copy.wait_send()
    for c in range(4):
        side_copies[c].wait_send()
        low0_copies[c].wait_send()


def slot_sources(tiles, grp):
    rows = tiles.shape[0]
    order = jnp.arange(rows, dtype=jnp.int32)
    come = order // PER
    dy = (grp // 2 - come // 2) % N_Y
    step = ((dy - 1) % N_Y) * 2 + 1 - (grp - come) % 2
    unit = step * UNITS + order % PER
    same = tiles[:, None] == tiles[None, :]
    rank = jnp.sum(jnp.where(same & (order[None, :] < order[:, None]), 1, 0), axis=1)
    slot_of = tiles * CT + rank.astype(jnp.int32)
    match = jnp.arange(N_TILE * CT, dtype=jnp.int32)[:, None] == slot_of[None, :]
    return PER + jnp.sum(jnp.where(match, unit[None, :] - PER, 0), axis=1)


def shards(
    visibilities,
    channel_taps,
    time_taps,
    channel_shift,
    time_shift,
    corner,
    plane_index,
    owner_tile,
):
    rows = visibilities.shape[2]
    source = slot_sources(owner_tile[0, 0], lax.axis_index("grp"))
    smem = pl.BlockSpec(memory_space=pltpu.SMEM)
    vmem = pl.BlockSpec(memory_space=pltpu.VMEM)
    hbm = pl.BlockSpec(memory_space=pl.ANY)
    dma = pltpu.SemaphoreType.DMA
    return pl.pallas_call(
        grid_kernel,
        out_shape=jax.ShapeDtypeStruct((PLANES, 2, TILE, TILE), f32),
        in_specs=[smem, smem, smem, hbm, hbm, hbm, vmem, vmem],
        out_specs=vmem,
        scratch_shapes=[
            pltpu.VMEM((rows, TM, 2 * CH), bf16),
            pltpu.VMEM((rows * 8, CH), bf16),
            pltpu.VMEM((rows, CH), jnp.int32),
            pltpu.VMEM((N_GRP * UNITS, TM, 128), bf16),
            pltpu.VMEM((N_GRP * UNITS, TM, 128), bf16),
            pltpu.VMEM((N_GRP * UNITS, MROWS, 128), f32),
            pltpu.VMEM((N_TILE, PROWS, 128), bf16),
            pltpu.VMEM((N_TILE, PROWS, 128), bf16),
            pltpu.VMEM((12, 384, 128), f32),
            pltpu.VMEM((4, 384, 128), f32),
            pltpu.VMEM((4, 128, 128), f32),
            pltpu.VMEM((4, 128, 128), f32),
            dma((N_GRP,)),
            dma((2,)),
            dma((N_GRP,)),
            dma((N_GRP,)),
            dma((N_TILE,)),
            dma((N_TILE,)),
            dma((2, 4)),
            dma((2, 4)),
            dma((2,)),
        ],
        compiler_params=pltpu.CompilerParams(
            collective_id=0, has_side_effects=True, vmem_limit_bytes=44 * 1024 * 1024
        ),
    )(
        corner[0, 0],
        plane_index[0, 0],
        source,
        visibilities[0, 0],
        channel_taps[0, 0].reshape(rows * 8, CH),
        channel_shift[0, 0],
        time_taps[0, 0],
        time_shift[0, 0],
    )


def solution(mesh):
    in_specs = (
        P("tile", "grp", None, None, None),
        P("tile", "grp", None, None, None),
        P("tile", "grp", None, None, None),
        P("tile", "grp", None, None),
        P("tile", "grp", None, None),
        P("tile", "grp", None, None),
        P("tile", "grp", None),
        P("tile", "grp", None),
    )
    out_specs = P(None, None, "tile", "grp")
    return jax.shard_map(shards, mesh=mesh, in_specs=in_specs, out_specs=out_specs, check_vma=False)
```

```python
import jax
import jax.numpy as jnp
from jax import lax
from jax.experimental import pallas as pl
from jax.experimental.pallas import tpu as pltpu
from jax.sharding import PartitionSpec as P

PATCH = 64
TILE = 128
PLANES = 8
TM = 32
CH = 256
N_X = 4
N_Z = 16
N_Y = 4
N_TILE = N_X * N_Z
N_GRP = 2 * N_Y
PER = 8
UNITS = PER + 1
PROWS = 2 * TM + 8
SELF_G = N_GRP - 1
SELF_T = N_TILE - N_X
VMEM_BYTES = 60 * 1024 * 1024
MESH = pl.DeviceIdType.MESH
f32 = jnp.float32
bf16 = jnp.bfloat16


def rotated(taps, low):
    for bit in (1, 2, 4):
        taps = jnp.where((low & bit) != 0, pltpu.roll(taps, bit, 0), taps)
    return taps


def grp_at(grp, e, way):
    q = lax.div(e, 2)
    dy = lax.rem(2 + 3 * q + 3 * lax.div(q * (q + 7), 2), N_Y)
    dc = 1 - lax.rem(e, 2)
    y = lax.rem(lax.div(grp, 2) + way * dy + N_Y, N_Y)
    return y * 2 + lax.rem(lax.rem(grp, 2) + dc, 2)


def tile_at(tile, k, way):
    dx = lax.rem(k, N_X)
    zi = lax.div(k, N_X)
    half = lax.div(zi + 1, 2)
    dz = N_Z // 2 + half * (1 - 2 * lax.rem(zi, 2))
    x = lax.rem(lax.div(tile, N_Z) + way * dx + N_X, N_X)
    return x * N_Z + lax.rem(lax.rem(tile, N_Z) + way * dz + N_Z, N_Z)


def crossed(rows):
    sub = lax.broadcasted_iota(jnp.int32, (8, 128), 0) & 3
    group = lax.broadcasted_iota(jnp.int32, (8, 128), 1) >> 5
    out = jnp.where(sub == group, rows, 0.0)
    for d in range(1, 4):
        moved = jnp.where(sub >= d, pltpu.roll(rows, d, 0), pltpu.roll(rows, d + 4, 0))
        out = jnp.where(((sub - group) & 3) == d, pltpu.roll(moved, 128 - 32 * d, 1), out)
    return out


def place_batch(msgs, first):
    sub = lax.broadcasted_iota(jnp.int32, (8, 128), 0)
    prow = lax.broadcasted_iota(jnp.int32, (128, 128), 0) & (PATCH - 1)
    own = (sub == 0) | (sub == 1) | (sub == 4) | (sub == 5)
    lhs, rhs = [], []
    for q in range(2):
        a, b = first + 2 * q, first + 2 * q + 1
        ma = msgs[a, 2 * TM :, :].astype(f32)
        mb = msgs[b, 2 * TM :, :].astype(f32)
        taps = crossed(jnp.where(own, ma, pltpu.roll(mb, 2, 0)))
        ints = crossed(jnp.where(sub < 2, pltpu.roll(ma, 6, 0), mb)).astype(jnp.int32)
        at = jnp.broadcast_to(ints[0:1], (8, 128))
        level = jnp.broadcast_to(ints[2:3], (8, 128))
        low = at & 7
        turned = rotated(taps, low)
        group = (at >> 3) + jnp.where(sub < low, 1, 0)
        group = (group >> 3) * 64 + level * 8 + (group & 7)
        rhs.append(
            jnp.concatenate(
                [jnp.where(group == r, turned, 0.0).astype(bf16) for r in range(192)], axis=0
            )
        )
        g = jnp.concatenate([msgs[a, : 2 * TM, :], msgs[b, : 2 * TM, :]], axis=0)
        g = jnp.transpose(g.astype(f32))
        off = prow - ints[1:2]
        lhs.append(
            jnp.concatenate(
                [
                    jnp.where((off >= -64 * k) & (off < 64 - 64 * k), g, 0.0).astype(bf16)
                    for k in range(3)
                ],
                axis=0,
            )
        )
    return jnp.concatenate(lhs, axis=1), jnp.concatenate(rhs, axis=1)


def column_rows(ttaps, tshift, corner, plane):
    blocks = plane.shape[1]
    parts = [
        ttaps[...].astype(f32),
        (tshift[...] + corner[1:2, :]).astype(f32),
        jnp.broadcast_to(corner[0:1, :].astype(f32), (TM, blocks)),
        jnp.broadcast_to(plane[...].astype(f32), (TM, blocks)),
        jnp.zeros((TM, blocks), f32),
    ]
    rows = lax.broadcasted_iota(jnp.int32, (blocks, blocks), 0)
    cols = lax.broadcasted_iota(jnp.int32, (blocks, blocks), 1)
    one = jnp.where(rows == cols, 1.0, 0.0).astype(bf16)
    return lax.dot_general(
        one,
        jnp.concatenate(parts, axis=0).astype(bf16),
        (((1,), (1,)), ((), ())),
        preferred_element_type=f32,
    )


def slot_table(owner, grp):
    blocks = owner.shape[1]
    tile = lax.broadcasted_iota(jnp.int32, (N_TILE, 128), 0)
    order = lax.broadcasted_iota(jnp.int32, (N_TILE, 128), 1)
    row = jnp.concatenate([owner, jnp.full((1, 128 - blocks), -1, jnp.int32)], axis=1)
    match = jnp.broadcast_to(row, (N_TILE, 128)) == tile
    count = jnp.where(match, 1, 0)
    for step in (1, 2, 4, 8, 16, 32):
        count = count + jnp.where(order >= step, pltpu.roll(count, step, 1), 0)
    come = order >> 3
    dy = ((grp >> 1) - (come >> 1) + N_Y) & (N_Y - 1)
    q = jnp.where(dy == 2, 0, jnp.where(dy == 1, 1, jnp.where(dy == 3, 2, 3)))
    step = q * 2 + 1 - ((grp + come) & 1)
    unit = step * UNITS + (order & 7) + 1
    both = jnp.where(match, jnp.where(count == 1, unit, unit * 256), 0)
    for step in (1, 2, 4, 8, 16, 32):
        both = both + pltpu.roll(both, step, 1)
    both = both + pltpu.roll(both, 64, 1)
    slot = jnp.where(order == 0, both & 255, both >> 8)
    return jnp.where(slot == 0, PER, slot - 1)


def grid_kernel(
    owner,
    corner,
    plane,
    tshift,
    ttaps,
    cshift,
    ctaps,
    vis,
    out,
    owner_buf,
    corner_buf,
    plane_buf,
    ts_buf,
    tt_buf,
    cs_buf,
    ct_buf,
    vis_buf,
    column_buf,
    table_buf,
    source,
    gout,
    gin,
    meta_buf,
    tout,
    tin,
    acc,
    side_in,
    low0_in,
    low1_in,
    vis_sem,
    small_sem,
    gsend,
    grecv,
    tsend,
    trecv,
    side_sem,
    low0_sem,
    low1_sem,
):
    tile = lax.axis_index("tile")
    grp = lax.axis_index("grp")

    barrier = pltpu.get_barrier_semaphore()

    def greet_tile(k, _):
        @pl.when(k != SELF_T)
        def _():
            pl.semaphore_signal(
                barrier, inc=1, device_id=(tile_at(tile, k, 1), grp), device_id_type=MESH
            )

        return 0

    def greet_grp(e, _):
        pl.semaphore_signal(
            barrier, inc=1, device_id=(tile, grp_at(grp, e, 1)), device_id_type=MESH
        )
        return 0

    def vis_copy(e):
        base = pl.multiple_of(grp_at(grp, e, 1) * PER, PER)
        return pltpu.make_async_copy(
            vis.at[pl.ds(base, PER)], vis_buf.at[pl.ds(e * PER, PER)], vis_sem.at[e]
        )

    small = [
        pltpu.make_async_copy(src, dst, small_sem.at[i])
        for i, (src, dst) in enumerate(
            [
                (corner, corner_buf),
                (plane, plane_buf),
                (tshift, ts_buf),
                (ttaps, tt_buf),
                (cshift, cs_buf),
                (ctaps, ct_buf),
                (owner, owner_buf),
            ]
        )
    ]
    for copy in small:
        copy.start()

    def start_vis(e, _):
        vis_copy(e).start()
        return 0

    lax.fori_loop(0, N_GRP, start_vis, 0)
    lax.fori_loop(0, N_GRP - 1, greet_grp, 0)
    lax.fori_loop(0, N_TILE, greet_tile, 0)

    for copy in small:
        copy.wait()
    column_buf[...] = column_rows(tt_buf, ts_buf, corner_buf, plane_buf)
    table_buf[...] = slot_table(owner_buf[...], grp)
    table_copy = pltpu.make_async_copy(table_buf, source, small_sem.at[0])
    table_copy.start()

    sub = lax.broadcasted_iota(jnp.int32, (8, CH), 0)
    sub1 = lax.broadcasted_iota(jnp.int32, (8, 128), 0)

    def grp_copy(e):
        units = pl.ds(e * UNITS, UNITS)
        return pltpu.make_async_remote_copy(
            src_ref=gout.at[units],
            dst_ref=gin.at[units],
            send_sem=gsend.at[e],
            recv_sem=grecv.at[e],
            device_id=(tile, grp_at(grp, e, 1)),
            device_id_type=MESH,
        )

    def fold(e, _):
        base = pl.multiple_of(grp_at(grp, e, 1) * PER, PER)
        vis_copy(e).wait()
        columns = column_buf[pl.ds(base, PER), :]
        row = columns[:, CH + TM : CH + TM + 1].astype(jnp.int32)
        shifts = (cs_buf[pl.ds(base, PER), :] + row) & (PATCH - 1)
        for b in range(PER):
            at = jnp.broadcast_to(shifts[b : b + 1, :], (8, CH))
            low = at & 7
            if b % 2 == 0:
                two = ct_buf[pl.ds(pl.multiple_of(base * 8, 16) + b * 8, 16), :].astype(f32)
            turned = rotated(two[(b % 2) * 8 : (b % 2) * 8 + 8], low)
            group = ((at >> 3) + jnp.where(sub < low, 1, 0)) & 7
            rows = jnp.concatenate(
                [jnp.where(group == r, turned, 0.0) for r in range(PATCH // 8)], axis=0
            ).astype(bf16)
            samples = vis_buf[e * PER + b]
            both = jnp.concatenate([samples[:, :CH], samples[:, CH:]], axis=0)
            made = lax.dot_general(
                both, rows, (((1,), (1,)), ((), ())), preferred_element_type=f32
            )
            gout[e * UNITS + b] = jnp.concatenate([made[:TM], made[TM:]], axis=1).astype(bf16)
        parts = [columns[:, 128 * j : 128 * (j + 1)] for j in range(3)]
        gout[e * UNITS + PER] = jnp.concatenate(
            parts + [jnp.zeros((PER, 128), f32)], axis=0
        ).astype(bf16)

        return 0

    def send_grp(e, _):
        grp_copy(e).start()
        return 0

    lax.fori_loop(0, N_GRP, fold, 0)
    pl.semaphore_wait(barrier, N_TILE - 1 + N_GRP - 1)
    lax.fori_loop(0, N_GRP - 1, send_grp, 0)
    gin[SELF_G * UNITS :] = gout[SELF_G * UNITS :]
    acc[...] = jnp.zeros_like(acc)
    meta_buf[PER] = jnp.zeros((8, 128), f32)
    table_copy.wait()

    def spread(e, _):
        @pl.when(e != SELF_G)
        def _():
            grp_copy(e).wait_recv()

        eight = gin[e * UNITS + PER].astype(f32)
        for b in range(PER):
            rows = jnp.zeros((8, 128), f32)
            for j, to in enumerate((0, 4, 2)):
                part = pltpu.roll(eight[8 * j : 8 * (j + 1)], (to - b) % 8, 0)
                rows = jnp.where(sub1 == to, part, rows)
            meta_buf[e * UNITS + b] = rows
        return 0

    lax.fori_loop(0, N_GRP, spread, 0)

    def tile_copy(k):
        return pltpu.make_async_remote_copy(
            src_ref=tout.at[k],
            dst_ref=tin.at[k],
            send_sem=tsend.at[k],
            recv_sem=trecv.at[k],
            device_id=(tile_at(tile, k, 1), grp),
            device_id_type=MESH,
        )

    def pack(k, _):
        to = tile_at(tile, k, 1)
        a = jnp.clip(source[to, 0], 0, N_GRP * UNITS - 1)
        b = jnp.clip(source[to, 1], 0, N_GRP * UNITS - 1)
        tout[k, :TM, :] = gin[a]
        tout[k, TM : 2 * TM, :] = gin[b]
        meta = meta_buf[a] + pltpu.roll(meta_buf[b], 1, 0)
        tout[k, 2 * TM :, :] = meta.astype(bf16)

        @pl.when(k != SELF_T)
        def _():
            tile_copy(k).start()

        return 0

    lax.fori_loop(0, N_TILE, pack, 0)
    tin[SELF_T] = tout[SELF_T]

    def place(step, _):
        for i in range(4):

            @pl.when(step * 4 + i != SELF_T)
            def _():
                tile_copy(step * 4 + i).wait_recv()

        lhs, rhs = place_batch(tin, step * 4)
        for n in range(6):
            part = lax.dot_general(
                lhs,
                rhs[256 * n : 256 * (n + 1)],
                (((1,), (1,)), ((), ())),
                preferred_element_type=f32,
            )
            acc[2 * n] += part[:, :128]
            acc[2 * n + 1] += part[:, 128:]
        return 0

    lax.fori_loop(0, N_TILE // 4, place, 0)

    down = lax.rem(tile + 1, N_TILE)
    right = lax.rem(grp + 1, N_GRP)
    side_copies = [
        pltpu.make_async_remote_copy(
            src_ref=acc.at[8 + c],
            dst_ref=side_in.at[c],
            send_sem=side_sem.at[0, c],
            recv_sem=side_sem.at[1, c],
            device_id=(tile, right),
            device_id_type=MESH,
        )
        for c in range(4)
    ]
    low1_copy = pltpu.make_async_remote_copy(
        src_ref=acc.at[pl.ds(4, 4), pl.ds(256, 128)],
        dst_ref=low1_in,
        send_sem=low1_sem.at[0],
        recv_sem=low1_sem.at[1],
        device_id=(down, grp),
        device_id_type=MESH,
    )
    low0_copies = [
        pltpu.make_async_remote_copy(
            src_ref=acc.at[c, pl.ds(256, 128)],
            dst_ref=low0_in.at[c],
            send_sem=low0_sem.at[0, c],
            recv_sem=low0_sem.at[1, c],
            device_id=(down, grp),
            device_id_type=MESH,
        )
        for c in range(4)
    ]
    for copy in side_copies:
        copy.start()
    low1_copy.start()
    for c in range(4):
        side_copies[c].wait_recv()
        acc[c] += side_in[c]
        low0_copies[c].start()

    def write(c, k, left, rest):
        for n in range(2):
            cols = slice(64 * n, 64 * (n + 1))
            both = jnp.concatenate([left[:, cols], rest[:, cols]], axis=1)
            for x in range(2):
                out[2 * c + n, x, 64 * k : 64 * (k + 1), :] = both[64 * x : 64 * (x + 1)]

    for c in range(4):
        write(c, 1, acc[c, 128:256], acc[4 + c, 128:256])
    low1_copy.wait_recv()
    for c in range(4):
        low0_copies[c].wait_recv()
        write(c, 0, acc[c, :128] + low0_in[c], acc[4 + c, :128] + low1_in[c])

    def sent_grp(e, _):
        grp_copy(e).wait_send()
        return 0

    def sent_tile(k, _):
        @pl.when(k != SELF_T)
        def _():
            tile_copy(k).wait_send()

        return 0

    lax.fori_loop(0, N_GRP - 1, sent_grp, 0)
    lax.fori_loop(0, N_TILE, sent_tile, 0)
    low1_copy.wait_send()
    for c in range(4):
        side_copies[c].wait_send()
        low0_copies[c].wait_send()


def shards(
    visibilities,
    channel_taps,
    time_taps,
    channel_shift,
    time_shift,
    corner,
    plane_index,
    owner_tile,
):
    rows = visibilities.shape[2]
    hbm = pl.BlockSpec(memory_space=pl.ANY)
    dma = pltpu.SemaphoreType.DMA
    return pl.pallas_call(
        grid_kernel,
        out_shape=jax.ShapeDtypeStruct((PLANES, 2, TILE, TILE), f32),
        in_specs=[hbm] * 8,
        out_specs=pl.BlockSpec(memory_space=pltpu.VMEM),
        scratch_shapes=[
            pltpu.VMEM((1, rows), jnp.int32),
            pltpu.VMEM((2, rows), jnp.int32),
            pltpu.VMEM((1, rows), jnp.int32),
            pltpu.VMEM((TM, rows), jnp.int32),
            pltpu.VMEM((8 * TM, rows), bf16),
            pltpu.VMEM((rows, CH), jnp.int32),
            pltpu.VMEM((rows * 8, CH), bf16),
            pltpu.VMEM((rows, TM, 2 * CH), bf16),
            pltpu.VMEM((rows, CH + 128), f32),
            pltpu.VMEM((N_TILE, 128), jnp.int32),
            pltpu.SMEM((N_TILE, 128), jnp.int32),
            pltpu.VMEM((N_GRP * UNITS, TM, 128), bf16),
            pltpu.VMEM((N_GRP * UNITS, TM, 128), bf16),
            pltpu.VMEM((N_GRP * UNITS, 8, 128), f32),
            pltpu.VMEM((N_TILE, PROWS, 128), bf16),
            pltpu.VMEM((N_TILE, PROWS, 128), bf16),
            pltpu.VMEM((12, 384, 128), f32),
            pltpu.VMEM((4, 384, 128), f32),
            pltpu.VMEM((4, 128, 128), f32),
            pltpu.VMEM((4, 128, 128), f32),
            dma((N_GRP,)),
            dma((7,)),
            dma((N_GRP,)),
            dma((N_GRP,)),
            dma((N_TILE,)),
            dma((N_TILE,)),
            dma((2, 4)),
            dma((2, 4)),
            dma((2,)),
        ],
        compiler_params=pltpu.CompilerParams(
            collective_id=0, has_side_effects=True, vmem_limit_bytes=VMEM_BYTES
        ),
    )(
        owner_tile[0],
        corner[0, 0].T,
        plane_index[0],
        time_shift[0, 0].T,
        time_taps[0, 0].transpose(1, 2, 0).reshape(8 * TM, rows),
        channel_shift[0, 0],
        channel_taps[0, 0].reshape(rows * 8, CH),
        visibilities[0, 0],
    )


def solution(mesh):
    in_specs = (
        P("tile", "grp", None, None, None),
        P("tile", "grp", None, None, None),
        P("tile", "grp", None, None, None),
        P("tile", "grp", None, None),
        P("tile", "grp", None, None),
        P("tile", "grp", None, None),
        P("tile", "grp", None),
        P("tile", "grp", None),
    )
    out_specs = P(None, None, "tile", "grp")
    return jax.shard_map(shards, mesh=mesh, in_specs=in_specs, out_specs=out_specs, check_vma=False)
```

```python
import jax
import jax.numpy as jnp
from jax import lax
from jax.experimental import pallas as pl
from jax.experimental.pallas import tpu as pltpu
from jax.sharding import PartitionSpec as P

PATCH = 64
TILE = 128
PLANES = 8
TM = 32
CH = 256
N_X = 4
N_Z = 16
N_Y = 4
N_TILE = N_X * N_Z
N_GRP = 2 * N_Y
PER = 8
HALF = TM // 2
UNITS = PER + 2
BROWS = TM + 8
SELF_G = N_GRP - 1
SELF_T = N_X
VMEM_BYTES = 60 * 1024 * 1024
MESH = pl.DeviceIdType.MESH
f32 = jnp.float32
bf16 = jnp.bfloat16


def rotated(taps, low):
    for bit in (1, 2, 4):
        taps = jnp.where((low & bit) != 0, pltpu.roll(taps, bit, 0), taps)
    return taps


def grp_at(grp, e, way):
    q = lax.div(e, 2)
    dy = lax.rem(2 + 3 * q + 3 * lax.div(q * (q + 7), 2), N_Y)
    dc = 1 - lax.rem(e, 2)
    y = lax.rem(lax.div(grp, 2) + way * dy + N_Y, N_Y)
    return y * 2 + lax.rem(lax.rem(grp, 2) + dc, 2)


def tile_at(tile, k, way):
    dx = lax.rem(k, N_X)
    zi = lax.div(k, N_X)
    i = lax.div(zi, 2)
    half = lax.div(i + 1, 2)
    dz = N_Z // 2 + half * (1 - 2 * lax.rem(i, 2)) + N_Z // 2 * lax.rem(zi, 2)
    x = lax.rem(lax.div(tile, N_Z) + way * dx + N_X, N_X)
    return x * N_Z + lax.rem(lax.rem(tile, N_Z) + way * dz + N_Z, N_Z)


def crossed(rows):
    sub = lax.broadcasted_iota(jnp.int32, (8, 128), 0) & 3
    group = lax.broadcasted_iota(jnp.int32, (8, 128), 1) >> 5
    out = jnp.where(sub == group, rows, 0.0)
    for d in range(1, 4):
        moved = jnp.where(sub >= d, pltpu.roll(rows, d, 0), pltpu.roll(rows, d + 4, 0))
        out = jnp.where(((sub - group) & 3) == d, pltpu.roll(moved, 128 - 32 * d, 1), out)
    return out


def place_batch(msgs_a, msgs_b, first):
    sub = lax.broadcasted_iota(jnp.int32, (8, 128), 0)
    prow = lax.broadcasted_iota(jnp.int32, (128, 128), 0) & (PATCH - 1)
    own = (sub == 0) | (sub == 1) | (sub == 4) | (sub == 5)
    lhs, rhs = [], []
    for q in range(2):
        a, b = first + 2 * q, first + 2 * q + 1
        ma = msgs_b[a, TM:, :].astype(f32)
        mb = msgs_b[b, TM:, :].astype(f32)
        taps = crossed(jnp.where(own, ma, pltpu.roll(mb, 2, 0)))
        ints = crossed(jnp.where(sub < 2, pltpu.roll(ma, 6, 0), mb)).astype(jnp.int32)
        at = jnp.broadcast_to(ints[0:1], (8, 128))
        level = jnp.broadcast_to(ints[2:3], (8, 128))
        low = at & 7
        turned = rotated(taps, low)
        group = (at >> 3) + jnp.where(sub < low, 1, 0)
        group = (group >> 3) * 64 + level * 8 + (group & 7)
        rhs.append(
            jnp.concatenate(
                [jnp.where(group == r, turned, 0.0).astype(bf16) for r in range(192)], axis=0
            )
        )
        g = jnp.concatenate(
            [
                part[m, HALF * slot : HALF * (slot + 1), :]
                for m in (a, b)
                for slot in range(2)
                for part in (msgs_a, msgs_b)
            ],
            axis=0,
        )
        g = jnp.transpose(g.astype(f32))
        off = prow - ints[1:2]
        lhs.append(
            jnp.concatenate(
                [
                    jnp.where((off >= -64 * k) & (off < 64 - 64 * k), g, 0.0).astype(bf16)
                    for k in range(3)
                ],
                axis=0,
            )
        )
    return jnp.concatenate(lhs, axis=1), jnp.concatenate(rhs, axis=1)


def column_rows(ttaps, tshift, corner, plane):
    blocks = plane.shape[1]
    parts = [
        ttaps[...].astype(f32),
        (tshift[...] + corner[1:2, :]).astype(f32),
        jnp.broadcast_to(corner[0:1, :].astype(f32), (TM, blocks)),
        jnp.broadcast_to(plane[...].astype(f32), (TM, blocks)),
        jnp.zeros((TM, blocks), f32),
    ]
    rows = lax.broadcasted_iota(jnp.int32, (blocks, blocks), 0)
    cols = lax.broadcasted_iota(jnp.int32, (blocks, blocks), 1)
    one = jnp.where(rows == cols, 1.0, 0.0).astype(bf16)
    return lax.dot_general(
        one,
        jnp.concatenate(parts, axis=0).astype(bf16),
        (((1,), (1,)), ((), ())),
        preferred_element_type=f32,
    )


def slot_table(owner, grp):
    blocks = owner.shape[1]
    tile = lax.broadcasted_iota(jnp.int32, (N_TILE, 128), 0)
    order = lax.broadcasted_iota(jnp.int32, (N_TILE, 128), 1)
    row = jnp.concatenate([owner, jnp.full((1, 128 - blocks), -1, jnp.int32)], axis=1)
    match = jnp.broadcast_to(row, (N_TILE, 128)) == tile
    count = jnp.where(match, 1, 0)
    for step in (1, 2, 4, 8, 16, 32):
        count = count + jnp.where(order >= step, pltpu.roll(count, step, 1), 0)
    come = order >> 3
    dy = ((grp >> 1) - (come >> 1) + N_Y) & (N_Y - 1)
    q = jnp.where(dy == 2, 0, jnp.where(dy == 1, 1, jnp.where(dy == 3, 2, 3)))
    step = q * 2 + 1 - ((grp + come) & 1)
    unit = step * PER + (order & 7) + 1
    both = jnp.where(match, jnp.where(count == 1, unit, unit * 256), 0)
    for step in (1, 2, 4, 8, 16, 32):
        both = both + pltpu.roll(both, step, 1)
    both = both + pltpu.roll(both, 64, 1)
    slot = jnp.where(order == 0, both & 255, both >> 8)
    return jnp.where(slot == 0, N_GRP * PER, slot - 1)


def grid_kernel(
    owner,
    corner,
    plane,
    tshift,
    ttaps,
    cshift,
    ctaps,
    vis,
    out,
    owner_buf,
    corner_buf,
    plane_buf,
    ts_buf,
    tt_buf,
    cs_buf,
    ct_buf,
    vis_buf,
    column_buf,
    table_buf,
    source,
    gout_a,
    gout_b,
    gin_a,
    gin_b,
    meta_buf,
    tout_a,
    tout_b,
    tin_a,
    tin_b,
    acc,
    side_in,
    low0_in,
    low1_in,
    vis_sem,
    small_sem,
    gsend,
    grecv,
    tsend,
    trecv,
    side_sem,
    low0_sem,
    low1_sem,
):
    tile = lax.axis_index("tile")
    grp = lax.axis_index("grp")

    barrier = pltpu.get_barrier_semaphore()

    def greet_tile(k, _):
        @pl.when(k != SELF_T)
        def _():
            pl.semaphore_signal(
                barrier, inc=1, device_id=(tile_at(tile, k, 1), grp), device_id_type=MESH
            )

        return 0

    def greet_grp(e, _):
        pl.semaphore_signal(
            barrier, inc=1, device_id=(tile, grp_at(grp, e, 1)), device_id_type=MESH
        )
        return 0

    def vis_copy(e):
        base = pl.multiple_of(grp_at(grp, e, 1) * PER, PER)
        return pltpu.make_async_copy(
            vis.at[pl.ds(base, PER)], vis_buf.at[pl.ds(e * PER, PER)], vis_sem.at[e]
        )

    small = [
        pltpu.make_async_copy(src, dst, small_sem.at[i])
        for i, (src, dst) in enumerate(
            [
                (corner, corner_buf),
                (plane, plane_buf),
                (tshift, ts_buf),
                (ttaps, tt_buf),
                (cshift, cs_buf),
                (ctaps, ct_buf),
                (owner, owner_buf),
            ]
        )
    ]
    for copy in small:
        copy.start()

    def start_vis(e, _):
        vis_copy(e).start()
        return 0

    lax.fori_loop(0, N_GRP, start_vis, 0)
    lax.fori_loop(0, N_GRP - 1, greet_grp, 0)
    lax.fori_loop(0, N_TILE, greet_tile, 0, unroll=8)

    for copy in small:
        copy.wait()
    column_buf[...] = column_rows(tt_buf, ts_buf, corner_buf, plane_buf)
    table_buf[...] = slot_table(owner_buf[...], grp)
    table_copy = pltpu.make_async_copy(table_buf, source, small_sem.at[0])
    table_copy.start()

    sub = lax.broadcasted_iota(jnp.int32, (8, CH), 0)
    sub1 = lax.broadcasted_iota(jnp.int32, (8, 128), 0)

    def grp_copy(part, e):
        src, dst, count = ((gout_a, gin_a, PER), (gout_b, gin_b, UNITS))[part]
        units = pl.ds(e * count, count)
        return pltpu.make_async_remote_copy(
            src_ref=src.at[units],
            dst_ref=dst.at[units],
            send_sem=gsend.at[part, e],
            recv_sem=grecv.at[part, e],
            device_id=(tile, grp_at(grp, e, 1)),
            device_id_type=MESH,
        )

    def fold(e, _):
        base = pl.multiple_of(grp_at(grp, e, 1) * PER, PER)
        vis_copy(e).wait()
        columns = column_buf[pl.ds(base, PER), :]
        row = columns[:, CH + TM : CH + TM + 1].astype(jnp.int32)
        shifts = (cs_buf[pl.ds(base, PER), :] + row) & (PATCH - 1)
        for b in range(PER):
            at = jnp.broadcast_to(shifts[b : b + 1, :], (8, CH))
            low = at & 7
            if b % 2 == 0:
                two = ct_buf[pl.ds(pl.multiple_of(base * 8, 16) + b * 8, 16), :].astype(f32)
            turned = rotated(two[(b % 2) * 8 : (b % 2) * 8 + 8], low)
            group = ((at >> 3) + jnp.where(sub < low, 1, 0)) & 7
            rows = jnp.concatenate(
                [jnp.where(group == r, turned, 0.0) for r in range(PATCH // 8)], axis=0
            ).astype(bf16)
            samples = vis_buf[e * PER + b]
            both = jnp.concatenate([samples[:, :CH], samples[:, CH:]], axis=0)
            made = lax.dot_general(
                both, rows, (((1,), (1,)), ((), ())), preferred_element_type=f32
            )
            made = jnp.concatenate([made[:TM], made[TM:]], axis=1).astype(bf16)
            gout_a[e * PER + b] = made[:HALF]
            gout_b[e * UNITS + b] = made[HALF:]
        parts = [columns[:, 128 * j : 128 * (j + 1)] for j in range(3)]
        gout_b[e * UNITS + PER] = jnp.concatenate(parts[:2], axis=0).astype(bf16)
        gout_b[e * UNITS + PER + 1] = jnp.concatenate(
            [parts[2], jnp.zeros((PER, 128), f32)], axis=0
        ).astype(bf16)
        return 0

    lax.fori_loop(0, N_GRP, fold, 0)
    pl.semaphore_wait(barrier, N_TILE - 1 + N_GRP - 1)
    for part in range(2):
        lax.fori_loop(0, N_GRP - 1, lambda e, _: (grp_copy(part, e).start(), 0)[1], 0)
    gin_a[SELF_G * PER :] = gout_a[SELF_G * PER :]
    gin_b[SELF_G * UNITS :] = gout_b[SELF_G * UNITS :]
    acc[...] = jnp.zeros_like(acc)
    meta_buf[N_GRP * PER] = jnp.zeros((8, 128), f32)
    table_copy.wait()

    def spread(e, _):
        @pl.when(e != SELF_G)
        def _():
            grp_copy(1, e).wait_recv()

        eight = jnp.concatenate([gin_b[e * UNITS + PER], gin_b[e * UNITS + PER + 1]], axis=0)
        eight = eight.astype(f32)
        for b in range(PER):
            rows = jnp.zeros((8, 128), f32)
            for j, to in enumerate((0, 4, 2)):
                part = pltpu.roll(eight[8 * j : 8 * (j + 1)], (to - b) % 8, 0)
                rows = jnp.where(sub1 == to, part, rows)
            meta_buf[e * PER + b] = rows
        return 0

    def tile_copy(part, k):
        src, dst = ((tout_a, tin_a), (tout_b, tin_b))[part]
        return pltpu.make_async_remote_copy(
            src_ref=src.at[k],
            dst_ref=dst.at[k],
            send_sem=tsend.at[part, k],
            recv_sem=trecv.at[part, k],
            device_id=(tile_at(tile, k, 1), grp),
            device_id_type=MESH,
        )

    def slots(k):
        to = tile_at(tile, k, 1)
        pair = [jnp.clip(source[to, i], 0, N_GRP * PER) for i in range(2)]
        return pair, [jnp.minimum(u, N_GRP * PER - 1) for u in pair]

    def came_a(e, _):
        grp_copy(0, e).wait_recv()
        return 0

    def pack_a(k, _):
        _, units = slots(k)
        for i in range(2):
            tout_a[k, HALF * i : HALF * (i + 1), :] = gin_a[units[i]]

        @pl.when(k != SELF_T)
        def _():
            tile_copy(0, k).start()

        return 0

    def pack_b(k, _):
        pair, units = slots(k)
        for i in range(2):
            unit = units[i] + 2 * lax.div(units[i], PER)
            tout_b[k, HALF * i : HALF * (i + 1), :] = gin_b[unit]
        meta = meta_buf[pair[0]] + pltpu.roll(meta_buf[pair[1]], 1, 0)
        tout_b[k, TM:, :] = meta.astype(bf16)

        @pl.when(k != SELF_T)
        def _():
            tile_copy(1, k).start()

        return 0

    lax.fori_loop(0, N_GRP - 1, came_a, 0)
    lax.fori_loop(0, N_TILE, pack_a, 0, unroll=4)
    lax.fori_loop(0, N_GRP, spread, 0, unroll=2)
    lax.fori_loop(0, N_TILE, pack_b, 0, unroll=4)
    tin_a[SELF_T] = tout_a[SELF_T]
    tin_b[SELF_T] = tout_b[SELF_T]

    def place(step, _):
        for i in range(4):

            @pl.when(step * 4 + i != SELF_T)
            def _():
                tile_copy(0, step * 4 + i).wait_recv()
                tile_copy(1, step * 4 + i).wait_recv()

        lhs, rhs = place_batch(tin_a, tin_b, step * 4)
        for n in range(6):
            part = lax.dot_general(
                lhs,
                rhs[256 * n : 256 * (n + 1)],
                (((1,), (1,)), ((), ())),
                preferred_element_type=f32,
            )
            acc[2 * n] += part[:, :128]
            acc[2 * n + 1] += part[:, 128:]
        return 0

    lax.fori_loop(0, N_TILE // 4, place, 0)

    down = lax.rem(tile + 1, N_TILE)
    right = lax.rem(grp + 1, N_GRP)
    side_copies = [
        pltpu.make_async_remote_copy(
            src_ref=acc.at[8 + c],
            dst_ref=side_in.at[c],
            send_sem=side_sem.at[0, c],
            recv_sem=side_sem.at[1, c],
            device_id=(tile, right),
            device_id_type=MESH,
        )
        for c in range(4)
    ]
    low1_copy = pltpu.make_async_remote_copy(
        src_ref=acc.at[pl.ds(4, 4), pl.ds(256, 128)],
        dst_ref=low1_in,
        send_sem=low1_sem.at[0],
        recv_sem=low1_sem.at[1],
        device_id=(down, grp),
        device_id_type=MESH,
    )
    low0_copies = [
        pltpu.make_async_remote_copy(
            src_ref=acc.at[c, pl.ds(256, 128)],
            dst_ref=low0_in.at[c],
            send_sem=low0_sem.at[0, c],
            recv_sem=low0_sem.at[1, c],
            device_id=(down, grp),
            device_id_type=MESH,
        )
        for c in range(4)
    ]
    for copy in side_copies:
        copy.start()
    low1_copy.start()
    for c in range(4):
        side_copies[c].wait_recv()
        acc[c] += side_in[c]
        low0_copies[c].start()

    def write(c, k, left, rest):
        for n in range(2):
            cols = slice(64 * n, 64 * (n + 1))
            both = jnp.concatenate([left[:, cols], rest[:, cols]], axis=1)
            for x in range(2):
                out[2 * c + n, x, 64 * k : 64 * (k + 1), :] = both[64 * x : 64 * (x + 1)]

    for c in range(4):
        write(c, 1, acc[c, 128:256], acc[4 + c, 128:256])
    low1_copy.wait_recv()
    for c in range(4):
        low0_copies[c].wait_recv()
        write(c, 0, acc[c, :128] + low0_in[c], acc[4 + c, :128] + low1_in[c])

    def sent_grp(e, _):
        grp_copy(0, e).wait_send()
        grp_copy(1, e).wait_send()
        return 0

    def sent_tile(k, _):
        @pl.when(k != SELF_T)
        def _():
            tile_copy(0, k).wait_send()
            tile_copy(1, k).wait_send()

        return 0

    lax.fori_loop(0, N_GRP - 1, sent_grp, 0)
    lax.fori_loop(0, N_TILE, sent_tile, 0, unroll=4)
    low1_copy.wait_send()
    for c in range(4):
        side_copies[c].wait_send()
        low0_copies[c].wait_send()


def shards(
    visibilities,
    channel_taps,
    time_taps,
    channel_shift,
    time_shift,
    corner,
    plane_index,
    owner_tile,
):
    rows = visibilities.shape[2]
    hbm = pl.BlockSpec(memory_space=pl.ANY)
    dma = pltpu.SemaphoreType.DMA
    return pl.pallas_call(
        grid_kernel,
        out_shape=jax.ShapeDtypeStruct((PLANES, 2, TILE, TILE), f32),
        in_specs=[hbm] * 8,
        out_specs=pl.BlockSpec(memory_space=pltpu.VMEM),
        scratch_shapes=[
            pltpu.VMEM((1, rows), jnp.int32),
            pltpu.VMEM((2, rows), jnp.int32),
            pltpu.VMEM((1, rows), jnp.int32),
            pltpu.VMEM((TM, rows), jnp.int32),
            pltpu.VMEM((8 * TM, rows), bf16),
            pltpu.VMEM((rows, CH), jnp.int32),
            pltpu.VMEM((rows * 8, CH), bf16),
            pltpu.VMEM((rows, TM, 2 * CH), bf16),
            pltpu.VMEM((rows, CH + 128), f32),
            pltpu.VMEM((N_TILE, 128), jnp.int32),
            pltpu.SMEM((N_TILE, 128), jnp.int32),
            pltpu.VMEM((N_GRP * PER, HALF, 128), bf16),
            pltpu.VMEM((N_GRP * UNITS, HALF, 128), bf16),
            pltpu.VMEM((N_GRP * PER, HALF, 128), bf16),
            pltpu.VMEM((N_GRP * UNITS, HALF, 128), bf16),
            pltpu.VMEM((N_GRP * PER + 1, 8, 128), f32),
            pltpu.VMEM((N_TILE, TM, 128), bf16),
            pltpu.VMEM((N_TILE, BROWS, 128), bf16),
            pltpu.VMEM((N_TILE, TM, 128), bf16),
            pltpu.VMEM((N_TILE, BROWS, 128), bf16),
            pltpu.VMEM((12, 384, 128), f32),
            pltpu.VMEM((4, 384, 128), f32),
            pltpu.VMEM((4, 128, 128), f32),
            pltpu.VMEM((4, 128, 128), f32),
            dma((N_GRP,)),
            dma((7,)),
            dma((2, N_GRP)),
            dma((2, N_GRP)),
            dma((2, N_TILE)),
            dma((2, N_TILE)),
            dma((2, 4)),
            dma((2, 4)),
            dma((2,)),
        ],
        compiler_params=pltpu.CompilerParams(
            collective_id=0, has_side_effects=True, vmem_limit_bytes=VMEM_BYTES
        ),
    )(
        owner_tile[0],
        corner[0, 0].T,
        plane_index[0],
        time_shift[0, 0].T,
        time_taps[0, 0].transpose(1, 2, 0).reshape(8 * TM, rows),
        channel_shift[0, 0],
        channel_taps[0, 0].reshape(rows * 8, CH),
        visibilities[0, 0],
    )


def solution(mesh):
    in_specs = (
        P("tile", "grp", None, None, None),
        P("tile", "grp", None, None, None),
        P("tile", "grp", None, None, None),
        P("tile", "grp", None, None),
        P("tile", "grp", None, None),
        P("tile", "grp", None, None),
        P("tile", "grp", None),
        P("tile", "grp", None),
    )
    out_specs = P(None, None, "tile", "grp")
    return jax.shard_map(shards, mesh=mesh, in_specs=in_specs, out_specs=out_specs, check_vma=False)
```

```python
import jax
import jax.numpy as jnp
from jax import lax
from jax.experimental import pallas as pl
from jax.experimental.pallas import tpu as pltpu
from jax.sharding import PartitionSpec as P

PATCH = 64
TILE = 128
PLANES = 8
TM = 32
CH = 256
N_X = 4
N_Z = 16
N_Y = 4
N_TILE = N_X * N_Z
N_GRP = 2 * N_Y
PER = 8
HALF = TM // 2
UNITS = PER + 2
BROWS = TM + 8
SELF_G = N_GRP - 1
SELF_T = N_TILE - N_X
VMEM_BYTES = 60 * 1024 * 1024
MESH = pl.DeviceIdType.MESH
f32 = jnp.float32
bf16 = jnp.bfloat16


def rotated(taps, low):
    for bit in (1, 2, 4):
        taps = jnp.where((low & bit) != 0, pltpu.roll(taps, bit, 0), taps)
    return taps


def grp_at(grp, e, way):
    q = lax.div(e, 2)
    dy = lax.rem(2 + 3 * q + 3 * lax.div(q * (q + 7), 2), N_Y)
    dc = 1 - lax.rem(e, 2)
    y = lax.rem(lax.div(grp, 2) + way * dy + N_Y, N_Y)
    return y * 2 + lax.rem(lax.rem(grp, 2) + dc, 2)


def tile_at(tile, k, way):
    dx = lax.rem(k, N_X)
    zi = lax.div(k, N_X)
    half = lax.div(zi + 1, 2)
    dz = N_Z // 2 + half * (1 - 2 * lax.rem(zi, 2))
    way = way * (1 - 2 * lax.rem(lax.axis_index("grp"), 2))
    x = lax.rem(lax.div(tile, N_Z) + way * dx + N_X, N_X)
    return x * N_Z + lax.rem(lax.rem(tile, N_Z) + way * dz + 2 * N_Z, N_Z)


def crossed(rows):
    sub = lax.broadcasted_iota(jnp.int32, (8, 128), 0) & 3
    group = lax.broadcasted_iota(jnp.int32, (8, 128), 1) >> 5
    out = jnp.where(sub == group, rows, 0.0)
    for d in range(1, 4):
        moved = jnp.where(sub >= d, pltpu.roll(rows, d, 0), pltpu.roll(rows, d + 4, 0))
        out = jnp.where(((sub - group) & 3) == d, pltpu.roll(moved, 128 - 32 * d, 1), out)
    return out


def place_batch(msgs_a, msgs_b, first):
    sub = lax.broadcasted_iota(jnp.int32, (8, 128), 0)
    prow = lax.broadcasted_iota(jnp.int32, (128, 128), 0) & (PATCH - 1)
    own = (sub == 0) | (sub == 1) | (sub == 4) | (sub == 5)
    lhs, rhs = [], []
    for q in range(2):
        a, b = first + 2 * q, first + 2 * q + 1
        ma = msgs_b[a, TM:, :].astype(f32)
        mb = msgs_b[b, TM:, :].astype(f32)
        taps = crossed(jnp.where(own, ma, pltpu.roll(mb, 2, 0)))
        ints = crossed(jnp.where(sub < 2, pltpu.roll(ma, 6, 0), mb)).astype(jnp.int32)
        at = jnp.broadcast_to(ints[0:1], (8, 128))
        level = jnp.broadcast_to(ints[2:3], (8, 128))
        low = at & 7
        turned = rotated(taps, low)
        group = (at >> 3) + jnp.where(sub < low, 1, 0)
        group = (group >> 3) * 64 + level * 8 + (group & 7)
        rhs.append(
            jnp.concatenate(
                [jnp.where(group == r, turned, 0.0).astype(bf16) for r in range(192)], axis=0
            )
        )
        g = jnp.concatenate(
            [
                part[m, HALF * slot : HALF * (slot + 1), :]
                for m in (a, b)
                for slot in range(2)
                for part in (msgs_a, msgs_b)
            ],
            axis=0,
        )
        g = jnp.transpose(g.astype(f32))
        off = prow - ints[1:2]
        lhs.append(
            jnp.concatenate(
                [
                    jnp.where((off >= -64 * k) & (off < 64 - 64 * k), g, 0.0).astype(bf16)
                    for k in range(3)
                ],
                axis=0,
            )
        )
    return jnp.concatenate(lhs, axis=1), jnp.concatenate(rhs, axis=1)


def column_rows(ttaps, tshift, corner, plane):
    blocks = plane.shape[1]
    parts = [
        ttaps[...].astype(f32),
        (tshift[...] + corner[1:2, :]).astype(f32),
        jnp.broadcast_to(corner[0:1, :].astype(f32), (TM, blocks)),
        jnp.broadcast_to(plane[...].astype(f32), (TM, blocks)),
        jnp.zeros((TM, blocks), f32),
    ]
    rows = lax.broadcasted_iota(jnp.int32, (blocks, blocks), 0)
    cols = lax.broadcasted_iota(jnp.int32, (blocks, blocks), 1)
    one = jnp.where(rows == cols, 1.0, 0.0).astype(bf16)
    return lax.dot_general(
        one,
        jnp.concatenate(parts, axis=0).astype(bf16),
        (((1,), (1,)), ((), ())),
        preferred_element_type=f32,
    )


def slot_table(owner, grp):
    blocks = owner.shape[1]
    tile = lax.broadcasted_iota(jnp.int32, (N_TILE, 128), 0)
    order = lax.broadcasted_iota(jnp.int32, (N_TILE, 128), 1)
    row = jnp.concatenate([owner, jnp.full((1, 128 - blocks), -1, jnp.int32)], axis=1)
    match = jnp.broadcast_to(row, (N_TILE, 128)) == tile
    count = jnp.where(match, 1, 0)
    for step in (1, 2, 4, 8, 16, 32):
        count = count + jnp.where(order >= step, pltpu.roll(count, step, 1), 0)
    come = order >> 3
    dy = ((grp >> 1) - (come >> 1) + N_Y) & (N_Y - 1)
    q = jnp.where(dy == 2, 0, jnp.where(dy == 1, 1, jnp.where(dy == 3, 2, 3)))
    step = q * 2 + 1 - ((grp + come) & 1)
    unit = step * PER + (order & 7) + 1
    both = jnp.where(match, jnp.where(count == 1, unit, unit * 256), 0)
    for step in (1, 2, 4, 8, 16, 32):
        both = both + pltpu.roll(both, step, 1)
    both = both + pltpu.roll(both, 64, 1)
    slot = jnp.where(order == 0, both & 255, both >> 8)
    return jnp.where(slot == 0, N_GRP * PER, slot - 1)


def grid_kernel(
    owner,
    corner,
    plane,
    tshift,
    ttaps,
    cshift,
    ctaps,
    vis,
    out,
    owner_buf,
    corner_buf,
    plane_buf,
    ts_buf,
    tt_buf,
    cs_buf,
    ct_buf,
    vis_buf,
    column_buf,
    table_buf,
    source,
    gout_a,
    gout_b,
    gin_a,
    gin_b,
    meta_buf,
    tout_a,
    tout_b,
    tin_a,
    tin_b,
    acc,
    side_out,
    side_in,
    side_cut,
    low_out,
    low_in,
    low_cut,
    vis_sem,
    small_sem,
    gsend,
    grecv,
    tsend,
    trecv,
    side_sem,
    low0_sem,
    low1_sem,
):
    tile = lax.axis_index("tile")
    grp = lax.axis_index("grp")

    barrier = pltpu.get_barrier_semaphore()

    def greet_tile(k, _):
        @pl.when(k != SELF_T)
        def _():
            pl.semaphore_signal(
                barrier, inc=1, device_id=(tile_at(tile, k, 1), grp), device_id_type=MESH
            )

        return 0

    def greet_grp(e, _):
        pl.semaphore_signal(
            barrier, inc=1, device_id=(tile, grp_at(grp, e, 1)), device_id_type=MESH
        )
        return 0

    def vis_copy(e):
        base = pl.multiple_of(grp_at(grp, e, 1) * PER, PER)
        return pltpu.make_async_copy(
            vis.at[pl.ds(base, PER)], vis_buf.at[pl.ds(e * PER, PER)], vis_sem.at[e]
        )

    small = [
        pltpu.make_async_copy(src, dst, small_sem.at[i])
        for i, (src, dst) in enumerate(
            [
                (corner, corner_buf),
                (plane, plane_buf),
                (tshift, ts_buf),
                (ttaps, tt_buf),
                (cshift, cs_buf),
                (ctaps, ct_buf),
                (owner, owner_buf),
            ]
        )
    ]
    for copy in small:
        copy.start()

    def start_vis(e, _):
        vis_copy(e).start()
        return 0

    lax.fori_loop(0, N_GRP, start_vis, 0)
    lax.fori_loop(0, N_GRP - 1, greet_grp, 0)
    lax.fori_loop(0, N_TILE, greet_tile, 0, unroll=8)

    for copy in small:
        copy.wait()
    column_buf[...] = column_rows(tt_buf, ts_buf, corner_buf, plane_buf)
    table_buf[...] = slot_table(owner_buf[...], grp)
    table_copy = pltpu.make_async_copy(table_buf, source, small_sem.at[0])
    table_copy.start()

    sub = lax.broadcasted_iota(jnp.int32, (8, CH), 0)
    sub1 = lax.broadcasted_iota(jnp.int32, (8, 128), 0)

    def grp_copy(part, e):
        src, dst, count = ((gout_a, gin_a, PER), (gout_b, gin_b, UNITS))[part]
        units = pl.ds(e * count, count)
        return pltpu.make_async_remote_copy(
            src_ref=src.at[units],
            dst_ref=dst.at[units],
            send_sem=gsend.at[part, e],
            recv_sem=grecv.at[part, e],
            device_id=(tile, grp_at(grp, e, 1)),
            device_id_type=MESH,
        )

    def fold(e, _):
        base = pl.multiple_of(grp_at(grp, e, 1) * PER, PER)
        vis_copy(e).wait()
        columns = column_buf[pl.ds(base, PER), :]
        row = columns[:, CH + TM : CH + TM + 1].astype(jnp.int32)
        shifts = (cs_buf[pl.ds(base, PER), :] + row) & (PATCH - 1)
        for b in range(PER):
            at = jnp.broadcast_to(shifts[b : b + 1, :], (8, CH))
            low = at & 7
            if b % 2 == 0:
                two = ct_buf[pl.ds(pl.multiple_of(base * 8, 16) + b * 8, 16), :].astype(f32)
            turned = rotated(two[(b % 2) * 8 : (b % 2) * 8 + 8], low)
            group = ((at >> 3) + jnp.where(sub < low, 1, 0)) & 7
            rows = jnp.concatenate(
                [jnp.where(group == r, turned, 0.0) for r in range(PATCH // 8)], axis=0
            ).astype(bf16)
            samples = vis_buf[e * PER + b]
            both = jnp.concatenate([samples[:, :CH], samples[:, CH:]], axis=0)
            made = lax.dot_general(
                both, rows, (((1,), (1,)), ((), ())), preferred_element_type=f32
            )
            made = jnp.concatenate([made[:TM], made[TM:]], axis=1).astype(bf16)
            gout_a[e * PER + b] = made[:HALF]
            gout_b[e * UNITS + b] = made[HALF:]
        parts = [columns[:, 128 * j : 128 * (j + 1)] for j in range(3)]
        gout_b[e * UNITS + PER] = jnp.concatenate(parts[:2], axis=0).astype(bf16)
        gout_b[e * UNITS + PER + 1] = jnp.concatenate(
            [parts[2], jnp.zeros((PER, 128), f32)], axis=0
        ).astype(bf16)
        return 0

    lax.fori_loop(0, N_GRP, fold, 0)
    pl.semaphore_wait(barrier, N_TILE - 1 + N_GRP - 1)
    for part in range(2):
        lax.fori_loop(0, N_GRP - 1, lambda e, _: (grp_copy(part, e).start(), 0)[1], 0)
    gin_a[SELF_G * PER :] = gout_a[SELF_G * PER :]
    gin_b[SELF_G * UNITS :] = gout_b[SELF_G * UNITS :]
    acc[...] = jnp.zeros_like(acc)
    meta_buf[N_GRP * PER] = jnp.zeros((8, 128), f32)
    table_copy.wait()

    def spread(e, _):
        @pl.when(e != SELF_G)
        def _():
            grp_copy(1, e).wait_recv()

        eight = jnp.concatenate([gin_b[e * UNITS + PER], gin_b[e * UNITS + PER + 1]], axis=0)
        eight = eight.astype(f32)
        for b in range(PER):
            rows = jnp.zeros((8, 128), f32)
            for j, to in enumerate((0, 4, 2)):
                part = pltpu.roll(eight[8 * j : 8 * (j + 1)], (to - b) % 8, 0)
                rows = jnp.where(sub1 == to, part, rows)
            meta_buf[e * PER + b] = rows
        return 0

    def tile_copy(part, k):
        src, dst = ((tout_a, tin_a), (tout_b, tin_b))[part]
        return pltpu.make_async_remote_copy(
            src_ref=src.at[k],
            dst_ref=dst.at[k],
            send_sem=tsend.at[part, k],
            recv_sem=trecv.at[part, k],
            device_id=(tile_at(tile, k, 1), grp),
            device_id_type=MESH,
        )

    def slots(k):
        to = tile_at(tile, k, 1)
        pair = [jnp.clip(source[to, i], 0, N_GRP * PER) for i in range(2)]
        return pair, [jnp.minimum(u, N_GRP * PER - 1) for u in pair]

    def came_a(e, _):
        grp_copy(0, e).wait_recv()
        return 0

    def pack_a(k, _):
        _, units = slots(k)
        for i in range(2):
            tout_a[k, HALF * i : HALF * (i + 1), :] = gin_a[units[i]]

        @pl.when(k != SELF_T)
        def _():
            tile_copy(0, k).start()

        return 0

    def pack_b(k, _):
        pair, units = slots(k)
        for i in range(2):
            unit = units[i] + 2 * lax.div(units[i], PER)
            tout_b[k, HALF * i : HALF * (i + 1), :] = gin_b[unit]
        meta = meta_buf[pair[0]] + pltpu.roll(meta_buf[pair[1]], 1, 0)
        tout_b[k, TM:, :] = meta.astype(bf16)

        @pl.when(k != SELF_T)
        def _():
            tile_copy(1, k).start()

        return 0

    lax.fori_loop(0, N_GRP - 1, came_a, 0)
    lax.fori_loop(0, N_TILE, pack_a, 0, unroll=4)
    lax.fori_loop(0, N_GRP, spread, 0, unroll=2)
    lax.fori_loop(0, N_TILE, pack_b, 0, unroll=4)
    tin_a[SELF_T] = tout_a[SELF_T]
    tin_b[SELF_T] = tout_b[SELF_T]

    def place(step, _):
        for i in range(4):

            @pl.when(step * 4 + i != SELF_T)
            def _():
                tile_copy(0, step * 4 + i).wait_recv()
                tile_copy(1, step * 4 + i).wait_recv()

        lhs, rhs = place_batch(tin_a, tin_b, step * 4)
        for n in range(6):
            part = lax.dot_general(
                lhs,
                rhs[256 * n : 256 * (n + 1)],
                (((1,), (1,)), ((), ())),
                preferred_element_type=f32,
            )
            acc[2 * n] += part[:, :128]
            acc[2 * n + 1] += part[:, 128:]
        return 0

    lax.fori_loop(0, N_TILE // 4, place, 0)

    down = lax.rem(tile + 1, N_TILE)
    right = lax.rem(grp + 1, N_GRP)
    def edge_copy(src, dst, sem, i, to):
        return pltpu.make_async_remote_copy(
            src_ref=src,
            dst_ref=dst,
            send_sem=sem.at[0, i],
            recv_sem=sem.at[1, i],
            device_id=to,
            device_id_type=MESH,
        )

    beside, below = (tile, right), (down, grp)
    low_rows = pl.ds(256, 128)
    side_copies = [
        edge_copy(acc.at[8 + c], side_in.at[c], side_sem, c, beside) for c in range(2)
    ] + [edge_copy(side_out.at[c], side_cut.at[c], side_sem, 2 + c, beside) for c in range(2)]
    low0_copies = [
        edge_copy(low_out.at[c], low_cut.at[c], low0_sem, c, below) for c in range(2)
    ] + [
        edge_copy(acc.at[2 + c, low_rows], low_in.at[c], low0_sem, 2 + c, below) for c in range(2)
    ]
    low1_copies = [
        edge_copy(low_out.at[pl.ds(2, 2)], low_cut.at[pl.ds(2, 2)], low1_sem, 0, below),
        edge_copy(acc.at[pl.ds(6, 2), low_rows], low_in.at[pl.ds(2, 2)], low1_sem, 1, below),
    ]
    order = (2, 3, 0, 1)
    side_out[...] = acc[10:].astype(bf16)
    for c in order:
        side_copies[c].start()
    low_out[2:] = acc[4:6, 256:].astype(bf16)
    for copy in low1_copies:
        copy.start()
    for c in order:
        side_copies[c].wait_recv()
        if c < 2:
            acc[c] += side_in[c]
            low_out[c] = acc[c, 256:].astype(bf16)
        else:
            acc[c] += side_cut[c - 2].astype(f32)
        low0_copies[c].start()

    def write(c, k, left, rest):
        for n in range(2):
            cols = slice(64 * n, 64 * (n + 1))
            both = jnp.concatenate([left[:, cols], rest[:, cols]], axis=1)
            for x in range(2):
                out[2 * c + n, x, 64 * k : 64 * (k + 1), :] = both[64 * x : 64 * (x + 1)]

    for c in range(4):
        write(c, 1, acc[c, 128:256], acc[4 + c, 128:256])
    for copy in low1_copies:
        copy.wait_recv()
    for c in order:
        low0_copies[c].wait_recv()
        if c < 2:
            low0, low1 = low_cut[c].astype(f32), low_cut[2 + c].astype(f32)
        else:
            low0, low1 = low_in[c - 2], low_in[c]
        write(c, 0, acc[c, :128] + low0, acc[4 + c, :128] + low1)

    def sent_grp(e, _):
        grp_copy(0, e).wait_send()
        grp_copy(1, e).wait_send()
        return 0

    def sent_tile(k, _):
        @pl.when(k != SELF_T)
        def _():
            tile_copy(0, k).wait_send()
            tile_copy(1, k).wait_send()

        return 0

    lax.fori_loop(0, N_GRP - 1, sent_grp, 0)
    lax.fori_loop(0, N_TILE, sent_tile, 0, unroll=4)
    for copy in side_copies + low0_copies + low1_copies:
        copy.wait_send()


def shards(
    visibilities,
    channel_taps,
    time_taps,
    channel_shift,
    time_shift,
    corner,
    plane_index,
    owner_tile,
):
    rows = visibilities.shape[2]
    hbm = pl.BlockSpec(memory_space=pl.ANY)
    dma = pltpu.SemaphoreType.DMA
    return pl.pallas_call(
        grid_kernel,
        out_shape=jax.ShapeDtypeStruct((PLANES, 2, TILE, TILE), f32),
        in_specs=[hbm] * 8,
        out_specs=pl.BlockSpec(memory_space=pltpu.VMEM),
        scratch_shapes=[
            pltpu.VMEM((1, rows), jnp.int32),
            pltpu.VMEM((2, rows), jnp.int32),
            pltpu.VMEM((1, rows), jnp.int32),
            pltpu.VMEM((TM, rows), jnp.int32),
            pltpu.VMEM((8 * TM, rows), bf16),
            pltpu.VMEM((rows, CH), jnp.int32),
            pltpu.VMEM((rows * 8, CH), bf16),
            pltpu.VMEM((rows, TM, 2 * CH), bf16),
            pltpu.VMEM((rows, CH + 128), f32),
            pltpu.VMEM((N_TILE, 128), jnp.int32),
            pltpu.SMEM((N_TILE, 128), jnp.int32),
            pltpu.VMEM((N_GRP * PER, HALF, 128), bf16),
            pltpu.VMEM((N_GRP * UNITS, HALF, 128), bf16),
            pltpu.VMEM((N_GRP * PER, HALF, 128), bf16),
            pltpu.VMEM((N_GRP * UNITS, HALF, 128), bf16),
            pltpu.VMEM((N_GRP * PER + 1, 8, 128), f32),
            pltpu.VMEM((N_TILE, TM, 128), bf16),
            pltpu.VMEM((N_TILE, BROWS, 128), bf16),
            pltpu.VMEM((N_TILE, TM, 128), bf16),
            pltpu.VMEM((N_TILE, BROWS, 128), bf16),
            pltpu.VMEM((12, 384, 128), f32),
            pltpu.VMEM((2, 384, 128), bf16),
            pltpu.VMEM((2, 384, 128), f32),
            pltpu.VMEM((2, 384, 128), bf16),
            pltpu.VMEM((4, 128, 128), bf16),
            pltpu.VMEM((4, 128, 128), f32),
            pltpu.VMEM((4, 128, 128), bf16),
            dma((N_GRP,)),
            dma((7,)),
            dma((2, N_GRP)),
            dma((2, N_GRP)),
            dma((2, N_TILE)),
            dma((2, N_TILE)),
            dma((2, 4)),
            dma((2, 4)),
            dma((2, 2)),
        ],
        compiler_params=pltpu.CompilerParams(
            collective_id=0, has_side_effects=True, vmem_limit_bytes=VMEM_BYTES
        ),
    )(
        owner_tile[0],
        corner[0, 0].T,
        plane_index[0],
        time_shift[0, 0].T,
        time_taps[0, 0].transpose(1, 2, 0).reshape(8 * TM, rows),
        channel_shift[0, 0],
        channel_taps[0, 0].reshape(rows * 8, CH),
        visibilities[0, 0],
    )


def solution(mesh):
    in_specs = (
        P("tile", "grp", None, None, None),
        P("tile", "grp", None, None, None),
        P("tile", "grp", None, None, None),
        P("tile", "grp", None, None),
        P("tile", "grp", None, None),
        P("tile", "grp", None, None),
        P("tile", "grp", None),
        P("tile", "grp", None),
    )
    out_specs = P(None, None, "tile", "grp")
    return jax.shard_map(shards, mesh=mesh, in_specs=in_specs, out_specs=out_specs, check_vma=False)
```

```python
import jax
import jax.numpy as jnp
from jax import lax
from jax.experimental import pallas as pl
from jax.experimental.pallas import tpu as pltpu
from jax.sharding import PartitionSpec as P

PATCH = 64
TILE = 128
PLANES = 8
TM = 32
CH = 256
N_X = 4
N_Z = 16
N_Y = 4
N_TILE = N_X * N_Z
N_GRP = 2 * N_Y
PER = 8
HALF = TM // 2
UNITS = PER + 2
BROWS = TM + 8
SELF_G = N_GRP - 1
SELF_T = N_TILE - N_X
VMEM_BYTES = 60 * 1024 * 1024
MESH = pl.DeviceIdType.MESH
f32 = jnp.float32
bf16 = jnp.bfloat16


def rotated(taps, low):
    for bit in (1, 2, 4):
        taps = jnp.where((low & bit) != 0, pltpu.roll(taps, bit, 0), taps)
    return taps


def grp_at(grp, e, way):
    q = lax.div(e, 2)
    dy = lax.rem(2 + 3 * q + 3 * lax.div(q * (q + 7), 2), N_Y)
    dc = 1 - lax.rem(e, 2)
    y = lax.rem(lax.div(grp, 2) + way * dy + N_Y, N_Y)
    return y * 2 + lax.rem(lax.rem(grp, 2) + dc, 2)


def tile_at(tile, k, way):
    dx = lax.rem(k, N_X)
    zi = lax.div(k, N_X)
    half = lax.div(zi + 1, 2)
    dz = N_Z // 2 + half * (1 - 2 * lax.rem(zi, 2))
    way = way * (1 - 2 * lax.rem(lax.axis_index("grp"), 2))
    x = lax.rem(lax.div(tile, N_Z) + way * dx + N_X, N_X)
    return x * N_Z + lax.rem(lax.rem(tile, N_Z) + way * dz + 2 * N_Z, N_Z)


def crossed(rows):
    sub = lax.broadcasted_iota(jnp.int32, (8, 128), 0) & 3
    group = lax.broadcasted_iota(jnp.int32, (8, 128), 1) >> 5
    out = jnp.where(sub == group, rows, 0.0)
    for d in range(1, 4):
        moved = jnp.where(sub >= d, pltpu.roll(rows, d, 0), pltpu.roll(rows, d + 4, 0))
        out = jnp.where(((sub - group) & 3) == d, pltpu.roll(moved, 128 - 32 * d, 1), out)
    return out


def place_batch(msgs_a, msgs_b, first):
    sub = lax.broadcasted_iota(jnp.int32, (8, 128), 0)
    prow = lax.broadcasted_iota(jnp.int32, (128, 128), 0) & (PATCH - 1)
    own = (sub == 0) | (sub == 1) | (sub == 4) | (sub == 5)
    lhs, rhs = [], []
    for q in range(2):
        a, b = first + 2 * q, first + 2 * q + 1
        ma = msgs_b[a, TM:, :].astype(f32)
        mb = msgs_b[b, TM:, :].astype(f32)
        taps = crossed(jnp.where(own, ma, pltpu.roll(mb, 2, 0)))
        ints = crossed(jnp.where(sub < 2, pltpu.roll(ma, 6, 0), mb)).astype(jnp.int32)
        at = jnp.broadcast_to(ints[0:1], (8, 128))
        level = jnp.broadcast_to(ints[2:3], (8, 128))
        low = at & 7
        turned = rotated(taps, low)
        group = (at >> 3) + jnp.where(sub < low, 1, 0)
        group = (group >> 3) * 64 + level * 8 + (group & 7)
        rhs.append(
            jnp.concatenate(
                [jnp.where(group == r, turned, 0.0).astype(bf16) for r in range(192)], axis=0
            )
        )
        g = jnp.concatenate(
            [
                part[m, HALF * slot : HALF * (slot + 1), :]
                for m in (a, b)
                for slot in range(2)
                for part in (msgs_a, msgs_b)
            ],
            axis=0,
        )
        g = jnp.transpose(g.astype(f32))
        off = prow - ints[1:2]
        lhs.append(
            jnp.concatenate(
                [
                    jnp.where((off >= -64 * k) & (off < 64 - 64 * k), g, 0.0).astype(bf16)
                    for k in range(3)
                ],
                axis=0,
            )
        )
    return jnp.concatenate(lhs, axis=1), jnp.concatenate(rhs, axis=1)


def column_rows(ttaps, tshift, corner, plane):
    blocks = plane.shape[1]
    parts = [
        ttaps[...].astype(f32),
        (tshift[...] + corner[1:2, :]).astype(f32),
        jnp.broadcast_to(corner[0:1, :].astype(f32), (TM, blocks)),
        jnp.broadcast_to(plane[...].astype(f32), (TM, blocks)),
        jnp.zeros((TM, blocks), f32),
    ]
    rows = lax.broadcasted_iota(jnp.int32, (blocks, blocks), 0)
    cols = lax.broadcasted_iota(jnp.int32, (blocks, blocks), 1)
    one = jnp.where(rows == cols, 1.0, 0.0).astype(bf16)
    return lax.dot_general(
        one,
        jnp.concatenate(parts, axis=0).astype(bf16),
        (((1,), (1,)), ((), ())),
        preferred_element_type=f32,
    )


def slot_table(owner, grp):
    blocks = owner.shape[1]
    tile = lax.broadcasted_iota(jnp.int32, (N_TILE, 128), 0)
    order = lax.broadcasted_iota(jnp.int32, (N_TILE, 128), 1)
    row = jnp.concatenate([owner, jnp.full((1, 128 - blocks), -1, jnp.int32)], axis=1)
    match = jnp.broadcast_to(row, (N_TILE, 128)) == tile
    count = jnp.where(match, 1, 0)
    for step in (1, 2, 4, 8, 16, 32):
        count = count + jnp.where(order >= step, pltpu.roll(count, step, 1), 0)
    come = order >> 3
    dy = ((grp >> 1) - (come >> 1) + N_Y) & (N_Y - 1)
    q = jnp.where(dy == 2, 0, jnp.where(dy == 1, 1, jnp.where(dy == 3, 2, 3)))
    step = q * 2 + 1 - ((grp + come) & 1)
    unit = step * PER + (order & 7) + 1
    both = jnp.where(match, jnp.where(count == 1, unit, unit * 256), 0)
    for step in (1, 2, 4, 8, 16, 32):
        both = both + pltpu.roll(both, step, 1)
    both = both + pltpu.roll(both, 64, 1)
    slot = jnp.where(order == 0, both & 255, both >> 8)
    return jnp.where(slot == 0, N_GRP * PER, slot - 1)


def grid_kernel(
    owner,
    corner,
    plane,
    tshift,
    ttaps,
    cshift,
    ctaps,
    vis,
    out,
    owner_buf,
    corner_buf,
    plane_buf,
    ts_buf,
    tt_buf,
    cs_buf,
    ct_buf,
    vis_buf,
    column_buf,
    table_buf,
    source,
    gout_a,
    gout_b,
    gin_a,
    gin_b,
    meta_buf,
    tout_a,
    tout_b,
    tin_a,
    tin_b,
    acc,
    side_out,
    side_in,
    side_cut,
    low_out,
    low_in,
    low_cut,
    out_buf,
    out_sem,
    vis_sem,
    small_sem,
    gsend,
    grecv,
    tsend,
    trecv,
    side_sem,
    low0_sem,
    low1_sem,
):
    tile = lax.axis_index("tile")
    grp = lax.axis_index("grp")

    barrier = pltpu.get_barrier_semaphore()

    def greet_tile(k, _):
        @pl.when(k != SELF_T)
        def _():
            pl.semaphore_signal(
                barrier, inc=1, device_id=(tile_at(tile, k, 1), grp), device_id_type=MESH
            )

        return 0

    def greet_grp(e, _):
        pl.semaphore_signal(
            barrier, inc=1, device_id=(tile, grp_at(grp, e, 1)), device_id_type=MESH
        )
        return 0

    def vis_copy(e):
        base = pl.multiple_of(grp_at(grp, e, 1) * PER, PER)
        return pltpu.make_async_copy(
            vis.at[pl.ds(base, PER)], vis_buf.at[pl.ds(e * PER, PER)], vis_sem.at[e]
        )

    small = [
        pltpu.make_async_copy(src, dst, small_sem.at[i])
        for i, (src, dst) in enumerate(
            [
                (corner, corner_buf),
                (plane, plane_buf),
                (tshift, ts_buf),
                (ttaps, tt_buf),
                (cshift, cs_buf),
                (ctaps, ct_buf),
                (owner, owner_buf),
            ]
        )
    ]
    for copy in small:
        copy.start()

    def start_vis(e, _):
        vis_copy(e).start()
        return 0

    lax.fori_loop(0, N_GRP, start_vis, 0)
    lax.fori_loop(0, N_GRP - 1, greet_grp, 0)
    lax.fori_loop(0, N_TILE, greet_tile, 0, unroll=8)

    for copy in small:
        copy.wait()
    column_buf[...] = column_rows(tt_buf, ts_buf, corner_buf, plane_buf)

    sub = lax.broadcasted_iota(jnp.int32, (8, CH), 0)
    sub1 = lax.broadcasted_iota(jnp.int32, (8, 128), 0)

    def grp_copy(part, e):
        src, dst, count = ((gout_a, gin_a, PER), (gout_b, gin_b, UNITS))[part]
        units = pl.ds(e * count, count)
        return pltpu.make_async_remote_copy(
            src_ref=src.at[units],
            dst_ref=dst.at[units],
            send_sem=gsend.at[part, e],
            recv_sem=grecv.at[part, e],
            device_id=(tile, grp_at(grp, e, 1)),
            device_id_type=MESH,
        )

    def fold(e, _):
        base = pl.multiple_of(grp_at(grp, e, 1) * PER, PER)
        vis_copy(e).wait()
        columns = column_buf[pl.ds(base, PER), :]
        row = columns[:, CH + TM : CH + TM + 1].astype(jnp.int32)
        shifts = (cs_buf[pl.ds(base, PER), :] + row) & (PATCH - 1)
        for b in range(PER):
            at = jnp.broadcast_to(shifts[b : b + 1, :], (8, CH))
            low = at & 7
            if b % 2 == 0:
                two = ct_buf[pl.ds(pl.multiple_of(base * 8, 16) + b * 8, 16), :].astype(f32)
            turned = rotated(two[(b % 2) * 8 : (b % 2) * 8 + 8], low)
            group = ((at >> 3) + jnp.where(sub < low, 1, 0)) & 7
            rows = jnp.concatenate(
                [jnp.where(group == r, turned, 0.0) for r in range(PATCH // 8)], axis=0
            ).astype(bf16)
            samples = vis_buf[e * PER + b]
            both = jnp.concatenate([samples[:, :CH], samples[:, CH:]], axis=0)
            made = lax.dot_general(
                both, rows, (((1,), (1,)), ((), ())), preferred_element_type=f32
            )
            made = jnp.concatenate([made[:TM], made[TM:]], axis=1).astype(bf16)
            gout_a[e * PER + b] = made[:HALF]
            gout_b[e * UNITS + b] = made[HALF:]
        parts = [columns[:, 128 * j : 128 * (j + 1)] for j in range(3)]
        gout_b[e * UNITS + PER] = jnp.concatenate(parts[:2], axis=0).astype(bf16)
        gout_b[e * UNITS + PER + 1] = jnp.concatenate(
            [parts[2], jnp.zeros((PER, 128), f32)], axis=0
        ).astype(bf16)
        return 0

    lax.fori_loop(0, N_GRP, fold, 0)
    pl.semaphore_wait(barrier, N_TILE - 1 + N_GRP - 1)
    for part in range(2):
        lax.fori_loop(0, N_GRP - 1, lambda e, _: (grp_copy(part, e).start(), 0)[1], 0)
    table_buf[...] = slot_table(owner_buf[...], grp)
    table_copy = pltpu.make_async_copy(table_buf, source, small_sem.at[0])
    table_copy.start()
    gin_a[SELF_G * PER :] = gout_a[SELF_G * PER :]
    gin_b[SELF_G * UNITS :] = gout_b[SELF_G * UNITS :]
    acc[...] = jnp.zeros_like(acc)
    meta_buf[N_GRP * PER] = jnp.zeros((8, 128), f32)
    table_copy.wait()

    def spread(e, _):
        @pl.when(e != SELF_G)
        def _():
            grp_copy(1, e).wait_recv()

        eight = jnp.concatenate([gin_b[e * UNITS + PER], gin_b[e * UNITS + PER + 1]], axis=0)
        eight = eight.astype(f32)
        for b in range(PER):
            rows = jnp.zeros((8, 128), f32)
            for j, to in enumerate((0, 4, 2)):
                part = pltpu.roll(eight[8 * j : 8 * (j + 1)], (to - b) % 8, 0)
                rows = jnp.where(sub1 == to, part, rows)
            meta_buf[e * PER + b] = rows
        return 0

    def tile_copy(part, k):
        src, dst = ((tout_a, tin_a), (tout_b, tin_b))[part]
        return pltpu.make_async_remote_copy(
            src_ref=src.at[k],
            dst_ref=dst.at[k],
            send_sem=tsend.at[part, k],
            recv_sem=trecv.at[part, k],
            device_id=(tile_at(tile, k, 1), grp),
            device_id_type=MESH,
        )

    def slots(k):
        to = tile_at(tile, k, 1)
        pair = [jnp.clip(source[to, i], 0, N_GRP * PER) for i in range(2)]
        return pair, [jnp.minimum(u, N_GRP * PER - 1) for u in pair]

    def came_a(e, _):
        grp_copy(0, e).wait_recv()
        return 0

    def pack_a(k, _):
        _, units = slots(k)
        for i in range(2):
            tout_a[k, HALF * i : HALF * (i + 1), :] = gin_a[units[i]]

        @pl.when(k != SELF_T)
        def _():
            tile_copy(0, k).start()

        return 0

    def pack_b(k, _):
        pair, units = slots(k)
        for i in range(2):
            unit = units[i] + 2 * lax.div(units[i], PER)
            tout_b[k, HALF * i : HALF * (i + 1), :] = gin_b[unit]
        meta = meta_buf[pair[0]] + pltpu.roll(meta_buf[pair[1]], 1, 0)
        tout_b[k, TM:, :] = meta.astype(bf16)

        @pl.when(k != SELF_T)
        def _():
            tile_copy(1, k).start()

        return 0

    lax.fori_loop(0, N_GRP - 1, came_a, 0)
    lax.fori_loop(0, N_TILE, pack_a, 0, unroll=4)
    lax.fori_loop(0, N_GRP, spread, 0, unroll=2)
    lax.fori_loop(0, N_TILE, pack_b, 0, unroll=4)
    tin_a[SELF_T] = tout_a[SELF_T]
    tin_b[SELF_T] = tout_b[SELF_T]

    def place(step, _):
        for i in range(4):

            @pl.when(step * 4 + i != SELF_T)
            def _():
                tile_copy(0, step * 4 + i).wait_recv()
                tile_copy(1, step * 4 + i).wait_recv()

        lhs, rhs = place_batch(tin_a, tin_b, step * 4)
        for n in range(6):
            part = lax.dot_general(
                lhs,
                rhs[256 * n : 256 * (n + 1)],
                (((1,), (1,)), ((), ())),
                preferred_element_type=f32,
            )
            acc[2 * n] += part[:, :128]
            acc[2 * n + 1] += part[:, 128:]
        return 0

    lax.fori_loop(0, N_TILE // 4, place, 0)

    down = lax.rem(tile + 1, N_TILE)
    right = lax.rem(grp + 1, N_GRP)
    def edge_copy(src, dst, sem, i, to):
        return pltpu.make_async_remote_copy(
            src_ref=src,
            dst_ref=dst,
            send_sem=sem.at[0, i],
            recv_sem=sem.at[1, i],
            device_id=to,
            device_id_type=MESH,
        )

    beside, below = (tile, right), (down, grp)
    low_rows = pl.ds(256, 128)
    side_copies = [
        edge_copy(acc.at[8 + c], side_in.at[c], side_sem, c, beside) for c in range(2)
    ] + [edge_copy(side_out.at[c], side_cut.at[c], side_sem, 2 + c, beside) for c in range(2)]
    low0_copies = [
        edge_copy(low_out.at[c], low_cut.at[c], low0_sem, c, below) for c in range(2)
    ] + [
        edge_copy(acc.at[2 + c, low_rows], low_in.at[c], low0_sem, 2 + c, below) for c in range(2)
    ]
    low1_copies = [
        edge_copy(low_out.at[pl.ds(2, 2)], low_cut.at[pl.ds(2, 2)], low1_sem, 0, below),
        edge_copy(acc.at[pl.ds(6, 2), low_rows], low_in.at[pl.ds(2, 2)], low1_sem, 1, below),
    ]
    order = (2, 3, 0, 1)
    side_out[...] = acc[10:].astype(bf16)
    for c in order:
        side_copies[c].start()
    low_out[2:] = acc[4:6, 256:].astype(bf16)
    for copy in low1_copies:
        copy.start()
    for c in order:
        side_copies[c].wait_recv()
        if c < 2:
            acc[c] += side_in[c]
            low_out[c] = acc[c, 256:].astype(bf16)
        else:
            acc[c] += side_cut[c - 2].astype(f32)
        low0_copies[c].start()

    def write(c, k, left, rest):
        for n in range(2):
            cols = slice(64 * n, 64 * (n + 1))
            both = jnp.concatenate([left[:, cols], rest[:, cols]], axis=1)
            for x in range(2):
                out_buf[2 * c + n, x, 64 * k : 64 * (k + 1), :] = both[64 * x : 64 * (x + 1)]

    for c in range(4):
        write(c, 1, acc[c, 128:256], acc[4 + c, 128:256])
    rows = pl.ds(64, 64)
    out_copies = [
        pltpu.make_async_copy(out_buf.at[:, :, rows], out.at[:, :, rows], out_sem.at[4])
    ]
    out_copies[0].start()
    for copy in low1_copies:
        copy.wait_recv()
    for c in order:
        low0_copies[c].wait_recv()
        if c < 2:
            low0, low1 = low_cut[c].astype(f32), low_cut[2 + c].astype(f32)
        else:
            low0, low1 = low_in[c - 2], low_in[c]
        write(c, 0, acc[c, :128] + low0, acc[4 + c, :128] + low1)
        part = (pl.ds(2 * c, 2), slice(None), pl.ds(0, 64))
        copy = pltpu.make_async_copy(out_buf.at[part], out.at[part], out_sem.at[c])
        copy.start()
        out_copies.append(copy)

    def sent_grp(e, _):
        grp_copy(0, e).wait_send()
        grp_copy(1, e).wait_send()
        return 0

    def sent_tile(k, _):
        @pl.when(k != SELF_T)
        def _():
            tile_copy(0, k).wait_send()
            tile_copy(1, k).wait_send()

        return 0

    lax.fori_loop(0, N_GRP - 1, sent_grp, 0)
    lax.fori_loop(0, N_TILE, sent_tile, 0, unroll=4)
    for copy in side_copies + low0_copies + low1_copies:
        copy.wait_send()
    for copy in out_copies:
        copy.wait()


def shards(
    visibilities,
    channel_taps,
    time_taps,
    channel_shift,
    time_shift,
    corner,
    plane_index,
    owner_tile,
):
    rows = visibilities.shape[2]
    hbm = pl.BlockSpec(memory_space=pl.ANY)
    dma = pltpu.SemaphoreType.DMA
    return pl.pallas_call(
        grid_kernel,
        out_shape=jax.ShapeDtypeStruct((PLANES, 2, TILE, TILE), f32),
        in_specs=[hbm] * 8,
        out_specs=hbm,
        scratch_shapes=[
            pltpu.VMEM((1, rows), jnp.int32),
            pltpu.VMEM((2, rows), jnp.int32),
            pltpu.VMEM((1, rows), jnp.int32),
            pltpu.VMEM((TM, rows), jnp.int32),
            pltpu.VMEM((8 * TM, rows), bf16),
            pltpu.VMEM((rows, CH), jnp.int32),
            pltpu.VMEM((rows * 8, CH), bf16),
            pltpu.VMEM((rows, TM, 2 * CH), bf16),
            pltpu.VMEM((rows, CH + 128), f32),
            pltpu.VMEM((N_TILE, 128), jnp.int32),
            pltpu.SMEM((N_TILE, 128), jnp.int32),
            pltpu.VMEM((N_GRP * PER, HALF, 128), bf16),
            pltpu.VMEM((N_GRP * UNITS, HALF, 128), bf16),
            pltpu.VMEM((N_GRP * PER, HALF, 128), bf16),
            pltpu.VMEM((N_GRP * UNITS, HALF, 128), bf16),
            pltpu.VMEM((N_GRP * PER + 1, 8, 128), f32),
            pltpu.VMEM((N_TILE, TM, 128), bf16),
            pltpu.VMEM((N_TILE, BROWS, 128), bf16),
            pltpu.VMEM((N_TILE, TM, 128), bf16),
            pltpu.VMEM((N_TILE, BROWS, 128), bf16),
            pltpu.VMEM((12, 384, 128), f32),
            pltpu.VMEM((2, 384, 128), bf16),
            pltpu.VMEM((2, 384, 128), f32),
            pltpu.VMEM((2, 384, 128), bf16),
            pltpu.VMEM((4, 128, 128), bf16),
            pltpu.VMEM((4, 128, 128), f32),
            pltpu.VMEM((4, 128, 128), bf16),
            pltpu.VMEM((PLANES, 2, TILE, TILE), f32),
            dma((5,)),
            dma((N_GRP,)),
            dma((7,)),
            dma((2, N_GRP)),
            dma((2, N_GRP)),
            dma((2, N_TILE)),
            dma((2, N_TILE)),
            dma((2, 4)),
            dma((2, 4)),
            dma((2, 2)),
        ],
        compiler_params=pltpu.CompilerParams(
            collective_id=0, has_side_effects=True, vmem_limit_bytes=VMEM_BYTES
        ),
    )(
        owner_tile[0],
        corner[0, 0].T,
        plane_index[0],
        time_shift[0, 0].T,
        time_taps[0, 0].transpose(1, 2, 0).reshape(8 * TM, rows),
        channel_shift[0, 0],
        channel_taps[0, 0].reshape(rows * 8, CH),
        visibilities[0, 0],
    )


def solution(mesh):
    in_specs = (
        P("tile", "grp", None, None, None),
        P("tile", "grp", None, None, None),
        P("tile", "grp", None, None, None),
        P("tile", "grp", None, None),
        P("tile", "grp", None, None),
        P("tile", "grp", None, None),
        P("tile", "grp", None),
        P("tile", "grp", None),
    )
    out_specs = P(None, None, "tile", "grp")
    return jax.shard_map(shards, mesh=mesh, in_specs=in_specs, out_specs=out_specs, check_vma=False)
```
